256 devices in a mesh: member: 8 (over x, core), space: 32 (over z, y).
Axes of the slice: x: 4, y: 4, z: 8, core: 2. Of those that a mesh axis runs over, the one named last changes fastest.
Arguments:
- inputs: bfloat16 [32, 512, 32768], P('member', None, 'space'), may hold values from -6 to 6
- w_in: bfloat16 [512, 512], P('space'), may hold values from -0.25 to 0.25
- bias_in: float32 [512], replicated, may hold values from -3 to 3
- w_out: bfloat16 [512, 87], P('space'), may hold values from -0.25 to 0.25
- members_out: float32 [32, 87, 32768], P('member', None, 'space'), may hold values from 0 to 16, as said below
- target: float32 [87, 32768], P(None, 'space'), may hold values from 0 to 16, as said below
- cell_area: float32 [32768], P('space'), may hold values from 0.5 to 1.5
Outputs:
- input_grad: bfloat16 [32, 512, 32768], P('member', None, 'space')
- w_in_grad: float32 [512, 512], P('space')
- w_out_grad: float32 [512, 87], P('space')
- bias_grad: float32 [512], P('space')
The draws below stay inside these ranges and needn't reach their ends.
Inputs may be any that keep to these rules, and one draw needn't show every extreme that they name: `members_out`: every value is an integer multiple of 2^-18; at each channel and cell the 32 members hold distinct values. `target`: every value is an odd multiple of 2^-19, so it never equals a member's value.
All inputs are finite; a program needn't handle non-finite values.
Results may differ from the reference program's by a relative error of at most 0.024.
Values may be sent and summed in bfloat16 or wider, within the bound.
A program may use at most 128 MiB of HBM per device.

```python
import math
import jax
import jax.numpy as jnp
from jax import lax

HID = 512
CHAN = 87
MEMBERS = 32
NCELLS = 32768


def cell_center(key):
    span_key, base_key = jax.random.split(jax.random.fold_in(key, 5))
    dims = (CHAN, NCELLS)
    exponent = jax.random.randint(span_key, dims, 0, 17)
    spread = jnp.left_shift(jnp.ones(dims, jnp.int32), exponent)
    center = jax.random.randint(base_key, dims, 0, 65537 - spread)
    return (center, spread)


def draw_members_out(key, part):
    center, spread = cell_center(key)
    key = jax.random.fold_in(key, 11)
    offset_key, order_key, fine_key = jax.random.split(key, 3)
    dims = (MEMBERS, CHAN, NCELLS)
    offset = jax.random.randint(offset_key, dims, 0, 65536) % spread[None]
    member_ids = lax.broadcasted_iota(jnp.int32, dims, 0)
    scores = jax.random.randint(order_key, dims, 0, 1048576) * 64 + member_ids
    order = jnp.argsort(scores, axis=0, stable=True).astype(jnp.int32)
    stride = 64 // MEMBERS
    lower = order * stride + jax.random.randint(fine_key, dims, 0, stride)
    whole = (center[None] + offset) * 64 + lower
    return whole.astype(jnp.float32) * 2.0 ** (-18)


def draw_target(key, part):
    center, spread = cell_center(key)
    key = jax.random.fold_in(key, 23)
    offset = jax.random.randint(key, (CHAN, NCELLS), 0, spread * 64)
    whole = (center * 64 + offset) * 2 + 1
    return whole.astype(jnp.float32) * 2.0 ** (-19)


def with_spikes(array, stream_key, source, target, shards_of, factor):
    owner, partner = [(jnp.arange(array.shape[axis_at]) // (array.shape[axis_at] // shards_of)).reshape([-1 if axis == axis_at else 1 for axis in range(array.ndim)]) for axis_at in (source, target)]
    chosen = jax.random.permutation(stream_key, shards_of)[partner]
    strong = (owner == chosen) | (owner == (partner + shards_of // 2) % shards_of)
    return jnp.where(strong, factor * array, array)


def block_levels(stream_key, shape, shards, low, largest):
    def one(dim, shards_of):
        steps = jax.random.uniform(jax.random.fold_in(jax.random.fold_in(stream_key, 6), dim), (shards_of,), jnp.float32, low / len(shards), largest / len(shards))
        return jnp.repeat(jnp.exp(steps), shape[dim] // shards_of).reshape((-1,) + (1,) * (len(shape) - dim - 1))

    gain = one(*shards[0])
    for cut in shards[1:]:
        gain = gain * one(*cut)
    return gain


def bell_draw(key, shape, deviation, bound, pieces=(), kind=jnp.bfloat16):
    loudness = block_levels(key, shape, pieces, -0.22, 0.18) if pieces else 1.0
    result = jax.random.normal(key, shape, jnp.float32) * deviation * loudness
    return jnp.minimum(jnp.maximum(result, -bound), bound).astype(kind)


def gaussian_with(key, shape, scale, limit, cuts, heavy, held_as=jnp.bfloat16):
    array = scale * jax.random.normal(key, shape, jnp.float32)
    if cuts:
        array = array * block_levels(key, shape, cuts, -0.22, 0.18)
    return jnp.clip(with_spikes(array, jax.random.fold_in(key, 3), *heavy), -limit, limit).astype(held_as)


def setup_inputs(seed: int = 0) -> dict:
    arg_keys = jax.random.split(jax.random.key(seed), 8)
    inputs = gaussian_with(arg_keys[0], (MEMBERS, HID, NCELLS), 1.0, 6.0, ((0, 8), (2, 32)), (2, 1, 32, 2.75))
    w_in = bell_draw(arg_keys[1], (HID, HID), HID ** -0.5, 0.25, ((0, 32),))
    bias_in = bell_draw(arg_keys[2], (HID,), 0.5, 3.0, (), jnp.float32)
    w_out = bell_draw(arg_keys[3], (HID, CHAN), HID ** -0.5, 0.25, ((0, 32),))
    members_out = draw_members_out(jax.random.fold_in(arg_keys[7], 71), 0)
    target = draw_target(jax.random.fold_in(arg_keys[7], 71), 0)
    cell_area = jnp.clip(0.5 + 1.0 * jax.random.uniform(arg_keys[6], (NCELLS,), jnp.float32) ** block_levels(arg_keys[6], (NCELLS,), ((0, 32),), -0.2, 0.2), 0.5, 1.5)
    return dict(inputs=inputs, w_in=w_in, bias_in=bias_in, w_out=w_out, members_out=members_out, target=target, cell_area=cell_area)


cubic_coef = 0.044715
root_coef = 0.7978845608028654

def gelu_parts(values):
    inner = root_coef * (values + cubic_coef * values * values * values)
    curve = jnp.tanh(inner)
    activated = 0.5 * values * (1.0 + curve)
    slope = 0.5 * (1.0 + curve) + 0.5 * values * (1.0 - curve * curve) * root_coef * (1.0 + 3.0 * cubic_coef * values * values)
    return (activated, slope)

def reference(inputs, w_in, bias_in, w_out, members_out, target, cell_area):
    member_count = members_out.shape[0]
    cell_count = members_out.shape[2]
    hidden_width = w_in.shape[0]
    chan_width = w_out.shape[1]
    target_sign = jnp.sign(members_out - target[None])

    def rank_row(member_row):
        return lax.optimization_barrier(jnp.sum(jnp.sign(member_row[None] - members_out), axis=0))
    rank_sums = lax.map(rank_row, members_out)
    grad_count = (member_count - 1) * target_sign - rank_sums
    out_grad = (grad_count * cell_area[None, None, :] / float(member_count)).astype(jnp.bfloat16)

    def member_step(running, pair):
        member_in, member_grad = pair
        pre_act = jnp.dot(w_in.T, member_in, preferred_element_type=jnp.float32) + bias_in[:, None]
        activated, slope = gelu_parts(pre_act)
        act_bf = activated.astype(jnp.bfloat16)
        act_grad = jnp.dot(w_out, member_grad, preferred_element_type=jnp.float32)
        pre_grad = (act_grad * slope).astype(jnp.bfloat16)
        input_grad = jnp.dot(w_in, pre_grad, preferred_element_type=jnp.float32).astype(jnp.bfloat16)
        sum_in = running[0] + jnp.dot(member_in, pre_grad.T, preferred_element_type=jnp.float32)
        sum_out = running[1] + jnp.dot(act_bf, member_grad.T, preferred_element_type=jnp.float32)
        sum_bias = running[2] + lax.optimization_barrier(jnp.sum(pre_grad.astype(jnp.float32), axis=1))
        return ((sum_in, sum_out, sum_bias), input_grad)
    initial = (jnp.zeros((hidden_width, hidden_width), jnp.float32), jnp.zeros((hidden_width, chan_width), jnp.float32), jnp.zeros((hidden_width,), jnp.float32))
    totals, input_grad = lax.scan(member_step, initial, (inputs, out_grad))
    grad_scale = 1.0 / math.sqrt(member_count * cell_count)
    return (input_grad, totals[0] * grad_scale, totals[1] * grad_scale, totals[2] * grad_scale)
```

```python
import functools
import math

import jax
import jax.numpy as jnp
from jax import lax
from jax.experimental import pallas as pl
from jax.experimental.pallas import tpu as pltpu
from jax.sharding import PartitionSpec as P

CUBIC = 0.044715
ROOT = 0.7978845608028654
MESH = pl.DeviceIdType.MESH
F32 = jnp.float32
BF16 = jnp.bfloat16
LANES = 128


def dot_nn(a, b):
    return jnp.dot(a, b, preferred_element_type=F32)


def dot_nt(a, b):
    return lax.dot_general(a, b, (((1,), (1,)), ((), ())), preferred_element_type=F32)


def kernel(
    members_n, spaces_n, chan, scale,
    x_hbm, w_hbm, bias_ref, wo_hbm, mem_hbm, tgt_hbm, area_ref,
    ig_hbm, win_out, wout_out, bias_out,
    x, w, wt, wo, wop, bias_b, got, last, tgt, back, og, act, slope, pg, ig,
    acc_in, acc_out, acc_b, part, pair, total, spread, owned, shares,
    load_sem, w_sem, w_send, a2a_recv, a2a_send, a2a_own, back_recv, back_send, back_own,
    pair_sem, red_recv, red_send, red_own, fin_recv, fin_send, fin_own, out_sem,
):
    me = lax.axis_index("member")
    here = lax.axis_index("space")
    core = lax.rem(me, 2)
    own_m, hid, cells = x.shape
    rows = w_hbm.shape[0]
    half_spaces = spaces_n // 2
    chips = members_n // 2
    count = own_m * members_n
    wide = acc_in.shape[1]

    def member_peer(k):
        return lax.rem(me + k, members_n)

    def space_peer(k):
        return lax.rem(here + k, spaces_n)

    barrier = pltpu.get_barrier_semaphore()

    def greet_space(k, _):
        pl.semaphore_signal(barrier, inc=1, device_id={"space": space_peer(k)}, device_id_type=MESH)
        return 0

    def greet_member(k, _):
        pl.semaphore_signal(barrier, inc=1, device_id={"member": member_peer(k)}, device_id_type=MESH)
        return 0

    loads = [pltpu.make_async_copy(x_hbm.at[m], x.at[m], load_sem.at[m]) for m in range(own_m)]
    own_cells = pl.ds(pl.multiple_of(me * LANES, LANES), LANES)
    tgt_load = pltpu.make_async_copy(tgt_hbm.at[:, own_cells], tgt, load_sem.at[own_m])
    lax.fori_loop(1, members_n, greet_member, 0)
    lax.fori_loop(1, spaces_n, greet_space, 0)
    tgt_load.start()
    pl.semaphore_wait(barrier, members_n + spaces_n - 2)

    cuts = ((0, 48), (48, chan))
    own_slots = pl.ds(pl.multiple_of(me * own_m, own_m), own_m)

    def values_to(k, part_at):
        lo, hi = cuts[part_at]
        peer = member_peer(k)
        return pltpu.make_async_remote_copy(
            src_ref=mem_hbm.at[:, lo:hi, pl.ds(pl.multiple_of(peer * LANES, LANES), LANES)],
            dst_ref=got.at[own_slots, lo:hi, :],
            send_sem=a2a_send.at[part_at],
            recv_sem=a2a_recv.at[part_at],
            device_id={"member": peer},
            device_id_type=MESH,
        )

    def own_values(part_at):
        lo, hi = cuts[part_at]
        return pltpu.make_async_copy(
            mem_hbm.at[:, lo:hi, own_cells], got.at[own_slots, lo:hi, :], a2a_own.at[part_at]
        )

    for part_at in range(2):
        for k in range(1, members_n):
            values_to(k, part_at).start()
        own_values(part_at).start()

    own_rows = pl.ds(pl.multiple_of(here * rows, rows), rows)

    def send_rows(k, _):
        peer = space_peer(k)
        pltpu.make_async_remote_copy(
            src_ref=w_hbm, dst_ref=w.at[own_rows, :], send_sem=w_send.at[0], recv_sem=w_sem.at[0],
            device_id={"space": peer}, device_id_type=MESH,
        ).start()
        pltpu.make_async_remote_copy(
            src_ref=wo_hbm, dst_ref=wo.at[own_rows, :], send_sem=w_send.at[1], recv_sem=w_sem.at[1],
            device_id={"space": peer}, device_id_type=MESH,
        ).start()
        return 0

    lax.fori_loop(1, spaces_n, send_rows, 0)
    own_w = pltpu.make_async_copy(w_hbm, w.at[own_rows, :], w_sem.at[2])
    own_wo = pltpu.make_async_copy(wo_hbm, wo.at[own_rows, :], w_sem.at[3])
    own_w.start()
    own_wo.start()
    for load in loads:
        load.start()

    bias_b[...] = jnp.broadcast_to(bias_ref[...], (LANES, hid)).T
    og[:, 96:, :] = jnp.zeros((own_m, og.shape[1] - 96, cells), BF16)
    wop[...] = jnp.zeros(wop.shape, BF16)
    last[...] = jnp.zeros(last.shape, F32)
    acc_in[...] = jnp.zeros(acc_in.shape, F32)
    acc_out[...] = jnp.zeros(acc_out.shape, F32)
    acc_b[...] = jnp.zeros(acc_b.shape, F32)

    tgt_load.wait()
    own_w.wait()
    own_wo.wait()
    others = (spaces_n - 1) * rows
    pltpu.make_async_copy(w.at[0:others, :], w.at[0:others, :], w_sem.at[0]).wait()
    pltpu.make_async_copy(wo.at[0:others, :], wo.at[0:others, :], w_sem.at[1]).wait()
    wt[...] = w[...].T
    wop[:, 0:chan] = wo[...]

    nb = 256
    blocks = cells // nb

    def forward(m):
        loads[m].wait()

        def step(b, _):
            at = pl.ds(pl.multiple_of(b * nb, nb), nb)
            bias2 = jnp.concatenate([bias_b[...]] * (nb // LANES), axis=1)
            v = dot_nn(wt[...], x[m, :, at]) + bias2
            sq = v * v
            u = 0.5 + 0.5 * jnp.tanh(v * (ROOT + (ROOT * CUBIC) * sq))
            a = v * u
            act[m, :, at] = a.astype(BF16)
            slope[m, :, at] = (u + a * (1.0 - u) * (2.0 * ROOT + (6.0 * ROOT * CUBIC) * sq)).astype(BF16)
            return 0

        lax.fori_loop(0, blocks, step, 0)

    area_row = area_ref[:, own_cells] * (1.0 / count)

    def rank_tile(load, target, store):
        values = [load(k) for k in range(count)]
        less = [None] * count
        for a in range(count):
            for b in range(a + 1, count):
                above = jnp.where(values[a] > values[b], 1.0, 0.0)
                less[a] = above if less[a] is None else less[a] + above
                less[b] = (float(b) - above) if less[b] is None else less[b] - above
        for a in range(count):
            grad = jnp.where(values[a] > target, float(2 * (count - 1)), 0.0) - 2.0 * less[a]
            store(a, grad * area_row)

    grads = spread

    def rank_rows(tile, _):
        at = pl.ds(pl.multiple_of(tile * 8, 8), 8)

        def store(k, value):
            grads[k, at, :] = value

        rank_tile(lambda k: got[k, at, :], tgt[at, :], store)
        return 0

    def pack(first, ending):
        def step(k, _):
            back[k, first:ending, :] = grads[k, first:ending, :].astype(BF16)
            return 0

        lax.fori_loop(0, count, step, 0)

    packs = ((0, 48), (48, 96))

    def grads_to(k, part_at):
        lo, hi = packs[part_at]
        peer = member_peer(k)
        return pltpu.make_async_remote_copy(
            src_ref=back.at[pl.ds(pl.multiple_of(peer * own_m, own_m), own_m), lo:hi, :],
            dst_ref=og.at[:, lo:hi, own_cells],
            send_sem=back_send.at[part_at],
            recv_sem=back_recv.at[part_at],
            device_id={"member": peer},
            device_id_type=MESH,
        )

    def own_grads(part_at):
        lo, hi = packs[part_at]
        return pltpu.make_async_copy(
            back.at[own_slots, lo:hi, :], og.at[:, lo:hi, own_cells], back_own.at[part_at]
        )

    def wait_values(part_at):
        lo, hi = cuts[part_at]
        own_values(part_at).wait()
        rest = got.at[0 : count - own_m, lo:hi, :]
        pltpu.make_async_copy(rest, rest, a2a_recv.at[part_at]).wait()

    def send_grads(part_at):
        for k in range(1, members_n):
            grads_to(k, part_at).start()
        own_grads(part_at).start()

    for m in range(own_m // 2):
        forward(m)
    wait_values(0)
    lax.fori_loop(0, 6, rank_rows, 0)
    pack(0, 48)
    send_grads(0)
    for m in range(own_m // 2, own_m):
        forward(m)
    wait_values(1)
    full = chan // 8
    lax.fori_loop(6, full, rank_rows, 0)
    tail = chan - full * 8
    for k in range(count):
        last[k, 0:tail, :] = got[k, full * 8 : chan, :]
    last[count, 0:tail, :] = tgt[full * 8 : chan, :]
    keep = lax.broadcasted_iota(jnp.int32, (8, LANES), 0) < tail

    def store_last(k, value):
        grads[k, full * 8 : full * 8 + 8, :] = jnp.where(keep, value, 0.0)
        grads[k, full * 8 + 8 : 96, :] = jnp.zeros((96 - full * 8 - 8, LANES), F32)

    rank_tile(lambda k: last[k], last[count], store_last)
    pack(48, 96)
    send_grads(1)

    for part_at in range(2):
        lo, hi = packs[part_at]
        own_grads(part_at).wait()
        rest = og.at[:, lo:hi, 0 : cells - LANES]
        pltpu.make_async_copy(rest, rest, back_recv.at[part_at]).wait()

    nc = 512

    def weight_terms(m, _):
        for b in range(cells // nc):
            at = slice(b * nc, (b + 1) * nc)
            p = dot_nn(wop[...], og[m, :, at]) * slope[m, :, at].astype(F32)
            pg[m, :, at] = p.astype(BF16)
            folded = p[:, 0:LANES]
            for c in range(1, nc // LANES):
                folded = folded + p[:, c * LANES : (c + 1) * LANES]
            acc_b[...] += folded
        acc_in[...] += dot_nt(x[m], pg[m])
        acc_out[...] += dot_nt(act[m], og[m])
        return 0

    lax.fori_loop(0, own_m, weight_terms, 0)

    lane = lax.broadcasted_iota(jnp.int32, (hid, LANES), 1)
    summed = jnp.sum(acc_b[...], axis=1, keepdims=True)
    acc_out[...] = jnp.where(lane == chan, summed, acc_out[...])

    half = hid // 2
    mine = pl.ds(pl.multiple_of(core * half, half), half)
    theirs = pl.ds(pl.multiple_of((1 - core) * half, half), half)
    part[:, 0:wide] = acc_in[theirs, :].astype(BF16)
    part[:, wide:] = acc_out[theirs, :].astype(BF16)
    sibling = me + 1 - 2 * core
    to_sibling = pltpu.make_async_remote_copy(
        src_ref=part, dst_ref=pair, send_sem=pair_sem.at[0], recv_sem=pair_sem.at[1],
        device_id={"member": sibling}, device_id_type=MESH,
    )
    to_sibling.start()

    def input_grads(m):
        def step(b, _):
            at = pl.ds(pl.multiple_of(b * nb, nb), nb)
            ig[m, :, at] = dot_nn(w[...], pg[m, :, at]).astype(BF16)
            return 0

        lax.fori_loop(0, blocks, step, 0)
        pltpu.make_async_copy(ig.at[m], ig_hbm.at[m], out_sem.at[m]).start()

    to_sibling.wait_recv()
    total[:, 0:wide] = (acc_in[mine, :] + pair[:, 0:wide].astype(F32)).astype(BF16)
    total[:, wide:] = (acc_out[mine, :] + pair[:, wide:].astype(F32)).astype(BF16)

    owner_core = here // half_spaces
    own_at = lax.rem(here, half_spaces)
    owner = owner_core == core

    def block_to(t):
        return pltpu.make_async_remote_copy(
            src_ref=total.at[pl.ds(pl.multiple_of(t * rows, rows), rows), :],
            dst_ref=shares.at[here],
            send_sem=red_send, recv_sem=red_recv,
            device_id={"space": core * half_spaces + t}, device_id_type=MESH,
        )

    own_block = pltpu.make_async_copy(
        total.at[pl.ds(pl.multiple_of(own_at * rows, rows), rows), :], shares.at[here], red_own
    )

    @pl.when(owner)
    def _():
        def send(k, _):
            block_to(lax.rem(own_at + k, half_spaces)).start()
            return 0

        lax.fori_loop(1, half_spaces, send, 0)
        own_block.start()

    @pl.when(jnp.logical_not(owner))
    def _():
        def send(k, _):
            block_to(lax.rem(own_at + k, half_spaces)).start()
            return 0

        lax.fori_loop(0, half_spaces, send, 0)

    for m in range(own_m - 1):
        input_grads(m)

    chip = me // 2

    def sum_to(k):
        return pltpu.make_async_remote_copy(
            src_ref=owned.at[chips], dst_ref=owned.at[chip], send_sem=fin_send, recv_sem=fin_recv,
            device_id={"member": member_peer(k)}, device_id_type=MESH,
        )

    own_sum = pltpu.make_async_copy(owned.at[chips], owned.at[chip], fin_own)

    @pl.when(owner)
    def _():
        own_block.wait()
        rest = shares.at[0 : spaces_n - 1]
        pltpu.make_async_copy(rest, rest, red_recv).wait()
        value = shares[0].astype(F32)
        for k in range(1, spaces_n):
            value = value + shares[k].astype(F32)
        owned[chips] = value.astype(BF16)
        for k in range(1, members_n):
            sum_to(k).start()
        own_sum.start()

    input_grads(own_m - 1)

    @pl.when(owner)
    def _():
        own_sum.wait()
        rest = owned.at[0 : chips - 1]
        pltpu.make_async_copy(rest, rest, fin_recv).wait()

    @pl.when(jnp.logical_not(owner))
    def _():
        rest = owned.at[0:chips]
        pltpu.make_async_copy(rest, rest, fin_recv).wait()

    result = owned[0].astype(F32)
    for k in range(1, chips):
        result = result + owned[k].astype(F32)
    result = result * scale
    win_out[...] = result[:, 0:wide]
    wout_out[...] = result[:, wide : wide + chan]
    column = result[:, wide + chan : wide + chan + 1]
    eye = lax.broadcasted_iota(jnp.int32, (rows, rows), 0) == lax.broadcasted_iota(jnp.int32, (rows, rows), 1)
    bias_out[...] = jnp.sum(jnp.where(eye, column, 0.0), axis=0, keepdims=True)

    for part_at in range(2):
        lo, hi = cuts[part_at]
        rest = got.at[0 : count - own_m, lo:hi, :]
        pltpu.make_async_copy(rest, rest, a2a_send.at[part_at]).wait()
        lo, hi = packs[part_at]
        rest = back.at[0 : count - own_m, lo:hi, :]
        pltpu.make_async_copy(rest, rest, back_send.at[part_at]).wait()
    pltpu.make_async_copy(w.at[0:others, :], w.at[0:others, :], w_send.at[0]).wait()
    pltpu.make_async_copy(wo.at[0:others, :], wo.at[0:others, :], w_send.at[1]).wait()
    to_sibling.wait_send()

    @pl.when(owner)
    def _():
        rest = total.at[0 : (half_spaces - 1) * rows, :]
        pltpu.make_async_copy(rest, rest, red_send).wait()
        rest = shares.at[0 : members_n - 1]
        pltpu.make_async_copy(rest, rest, fin_send).wait()

    @pl.when(jnp.logical_not(owner))
    def _():
        pltpu.make_async_copy(total, total, red_send).wait()

    for m in range(own_m):
        pltpu.make_async_copy(ig.at[m], ig_hbm.at[m], out_sem.at[m]).wait()


def body(members_n, spaces_n, inputs, w_in, bias_in, w_out, members_out, target, cell_area):
    own_m, hid, cells = inputs.shape
    rows, chan = w_out.shape
    count = own_m * members_n
    padded = LANES
    wide = w_in.shape[1]
    scale = 1.0 / math.sqrt(count * cells * spaces_n)
    chips = members_n // 2
    any_spec = pl.BlockSpec(memory_space=pl.ANY)
    vmem_spec = pl.BlockSpec(memory_space=pltpu.VMEM)
    dma = pltpu.SemaphoreType.DMA
    hidden = (own_m, hid, cells)
    outs = pl.pallas_call(
        functools.partial(kernel, members_n, spaces_n, chan, scale),
        out_shape=(
            jax.ShapeDtypeStruct(hidden, BF16),
            jax.ShapeDtypeStruct((rows, wide), F32),
            jax.ShapeDtypeStruct((rows, chan), F32),
            jax.ShapeDtypeStruct((1, rows), F32),
        ),
        in_specs=[any_spec, any_spec, vmem_spec, any_spec, any_spec, any_spec, vmem_spec],
        out_specs=(any_spec, vmem_spec, vmem_spec, vmem_spec),
        scratch_shapes=[
            pltpu.VMEM(hidden, BF16),
            pltpu.VMEM((hid, wide), BF16),
            pltpu.VMEM((wide, hid), BF16),
            pltpu.VMEM((hid, chan), BF16),
            pltpu.VMEM((hid, padded), BF16),
            pltpu.VMEM((hid, LANES), F32),
            pltpu.VMEM((count, chan, LANES), F32),
            pltpu.VMEM((count + 1, 8, LANES), F32),
            pltpu.VMEM((chan, LANES), F32),
            pltpu.VMEM((count, 96, LANES), BF16),
            pltpu.VMEM((own_m, padded, cells), BF16),
            pltpu.VMEM(hidden, BF16),
            pltpu.VMEM(hidden, BF16),
            pltpu.VMEM(hidden, BF16),
            pltpu.VMEM(hidden, BF16),
            pltpu.VMEM((hid, wide), F32),
            pltpu.VMEM((hid, LANES), F32),
            pltpu.VMEM((hid, LANES), F32),
            pltpu.VMEM((hid // 2, wide + LANES), BF16),
            pltpu.VMEM((hid // 2, wide + LANES), BF16),
            pltpu.VMEM((hid // 2, wide + LANES), BF16),
            pltpu.VMEM((count, 96, LANES), F32),
            pltpu.VMEM((chips + 1, rows, wide + LANES), BF16),
            pltpu.VMEM((spaces_n, rows, wide + LANES), BF16),
            dma((own_m + 1,)),
            dma((4,)),
            dma((2,)),
            dma((2,)),
            dma((2,)),
            dma((2,)),
            dma((2,)),
            dma((2,)),
            dma((2,)),
            dma((2,)),
            dma,
            dma,
            dma,
            dma,
            dma,
            dma,
            dma((own_m,)),
        ],
        compiler_params=pltpu.CompilerParams(
            collective_id=0, has_side_effects=True, vmem_limit_bytes=60 * 1024 * 1024
        ),
        name="crps_backward",
    )(
        inputs, w_in, bias_in.reshape(1, -1), w_out, members_out, target, cell_area.reshape(1, -1)
    )
    return outs[0], outs[1], outs[2], outs[3].reshape(rows)


def solution(mesh):
    members_n, spaces_n = mesh.shape["member"], mesh.shape["space"]
    return jax.shard_map(
        functools.partial(body, members_n, spaces_n),
        mesh=mesh,
        in_specs=(
            P("member", None, "space"),
            P("space", None),
            P(),
            P("space", None),
            P("member", None, "space"),
            P(None, "space"),
            P("space"),
        ),
        out_specs=(P("member", None, "space"), P("space", None), P("space", None), P("space")),
        check_vma=False,
    )
```

```python
import functools
import math

import jax
import jax.numpy as jnp
from jax import lax
from jax.experimental import pallas as pl
from jax.experimental.pallas import tpu as pltpu
from jax.sharding import PartitionSpec as P

CUBIC = 0.044715
ROOT = 0.7978845608028654
MESH = pl.DeviceIdType.MESH
F32 = jnp.float32
BF16 = jnp.bfloat16
LANES = 128
HALF_ROWS = 48


def dot_nn(a, b):
    return jnp.dot(a, b, preferred_element_type=F32)


def dot_nt(a, b):
    return lax.dot_general(a, b, (((1,), (1,)), ((), ())), preferred_element_type=F32)


def kernel(
    members_n, spaces_n, chan, scale,
    x_hbm, w_hbm, bias_hbm, wo_hbm, mem_hbm, tgt_hbm, area_hbm,
    ig, result_out,
    x, bias_ref, area_ref, stage, wo_raw, wo_wide, wall, wt, bias_b, got, flat, tgt_raw, tgt, grads, back, og, act, slope, pg,
    acc_in, acc_out, acc_b, part, pair, total, shares, owned,
    load_sem, w_recv, w_send, a2a_recv, a2a_send, a2a_own, back_recv, back_send, back_own,
    pair_sem, red_recv, red_send, fin_recv, fin_send,
):
    me = lax.axis_index("member")
    here = lax.axis_index("space")
    core = lax.rem(me, 2)
    own_m, hid, cells = x.shape
    rows = w_hbm.shape[0]
    half_spaces = spaces_n // 2
    half_members = members_n // 2
    half_hid = hid // 2
    half_cells = cells // 2
    count = own_m * members_n
    wide = wt.shape[0]
    half_chan = got.shape[2]
    my_half = lax.rem(here // half_spaces + core, 2)
    sibling = me + 1 - 2 * core

    def member_peer(k):
        return lax.rem(me + k, members_n)

    def space_peer(k):
        return my_half * half_spaces + lax.rem(here + k, half_spaces)

    barrier = pltpu.get_barrier_semaphore()

    def greet_space(k, _):
        pl.semaphore_signal(barrier, inc=1, device_id={"space": space_peer(k)}, device_id_type=MESH)
        return 0

    def greet_member(k, _):
        pl.semaphore_signal(barrier, inc=1, device_id={"member": member_peer(k)}, device_id_type=MESH)
        return 0

    first = 1 - core
    lax.fori_loop(first, half_spaces, greet_space, 0)
    lax.fori_loop(1, members_n, greet_member, 0)

    load_w = pltpu.make_async_copy(w_hbm, stage.at[:, 0:wide], load_sem.at[own_m])
    load_wo = pltpu.make_async_copy(wo_hbm, wo_raw, load_sem.at[own_m + 1])
    load_tgt = pltpu.make_async_copy(tgt_hbm, tgt_raw, load_sem.at[own_m + 2])
    load_bias = pltpu.make_async_copy(bias_hbm, bias_ref, load_sem.at[own_m + 3])
    load_area = pltpu.make_async_copy(area_hbm, area_ref, load_sem.at[own_m + 4])
    loads = [pltpu.make_async_copy(x_hbm.at[m], x.at[m], load_sem.at[m]) for m in range(own_m)]
    load_w.start()
    load_wo.start()
    load_tgt.start()
    load_bias.start()
    load_area.start()
    for load in loads:
        load.start()

    wo_wide[...] = jnp.zeros(wo_wide.shape, F32)
    load_wo.wait()
    wo_wide[:, 0:half_chan] = wo_raw[:, 0:half_chan].astype(F32)
    second = HALF_ROWS + 2 * half_chan - chan
    wo_wide[:, second : second + chan - half_chan] = wo_raw[:, half_chan:chan].astype(F32)
    stage[:, wide:] = wo_wide[...].astype(BF16)
    load_w.wait()

    pl.semaphore_wait(barrier, members_n - 1 + half_spaces - first)

    def place(peer, chunk):
        channel_half = lax.rem(peer // half_members + chunk, 2)
        tile = lax.rem(peer, half_members) + chunk * half_members
        return channel_half, pl.ds(pl.multiple_of(tile * LANES, LANES), LANES)

    def values_from(peer, chunk):
        channel_half, at = place(peer, chunk)
        return mem_hbm.at[pl.ds(channel_half * (chan - half_chan), half_chan), :, at]

    def values_to(k, chunk):
        peer = member_peer(k)
        return pltpu.make_async_remote_copy(
            src_ref=values_from(peer, chunk),
            dst_ref=got.at[chunk, me],
            send_sem=a2a_send.at[chunk],
            recv_sem=a2a_recv.at[chunk],
            device_id={"member": peer},
            device_id_type=MESH,
        )

    def own_values(chunk):
        return pltpu.make_async_copy(values_from(me, chunk), got.at[chunk, me], a2a_own.at[chunk])

    def send_values(chunk):
        for k in range(1, members_n):
            values_to(k, chunk).start()
        own_values(chunk).start()

    def send_rows(k, _):
        pltpu.make_async_remote_copy(
            src_ref=stage, dst_ref=wall.at[here], send_sem=w_send.at[0], recv_sem=w_recv.at[0],
            device_id={"space": space_peer(k)}, device_id_type=MESH,
        ).start()
        return 0

    send_values(0)
    lax.fori_loop(first, half_spaces, send_rows, 0)

    @pl.when(core == 0)
    def _():
        pltpu.make_async_copy(stage, wall.at[here], w_recv.at[0]).start()

    send_values(1)

    load_bias.wait()
    load_area.wait()
    bias_b[...] = jnp.broadcast_to(bias_ref[...], (LANES, hid)).T
    og[:, 2 * HALF_ROWS :, :] = jnp.zeros((own_m, og.shape[1] - 2 * HALF_ROWS, cells), BF16)
    flat[...] = jnp.zeros(flat.shape, F32)
    tgt[...] = jnp.zeros(tgt.shape, F32)
    acc_in[...] = jnp.zeros(acc_in.shape, F32)
    acc_out[...] = jnp.zeros(acc_out.shape, F32)
    acc_b[...] = jnp.zeros(acc_b.shape, F32)
    load_tgt.wait()
    tgt[0, 0:half_chan, :] = tgt_raw[0:half_chan, :]
    tgt[1, 0:half_chan, :] = tgt_raw[chan - half_chan : chan, :]

    mine_w = wall.at[pl.ds(my_half * half_spaces, half_spaces)]
    pltpu.make_async_copy(mine_w, mine_w, w_recv.at[0]).wait()
    pair_w = pltpu.make_async_remote_copy(
        src_ref=mine_w, dst_ref=mine_w, send_sem=w_send.at[1], recv_sem=w_recv.at[1],
        device_id={"member": sibling}, device_id_type=MESH,
    )
    pair_w.start()

    group = 8

    def rank(chunk):
        own_values(chunk).wait()
        rest = got.at[chunk, 0 : members_n - 1]
        pltpu.make_async_copy(rest, rest, a2a_recv.at[chunk]).wait()
        channel_half, at = place(me, chunk)
        area_row = area_ref[:, at] * (1.0 / count)

        def lay_out(source, _):
            for c in range(half_chan):
                flat[source, c * own_m : (c + 1) * own_m, :] = got[chunk, source, c]
            return 0

        lax.fori_loop(0, members_n, lay_out, 0)

        def rank_rows(tile, _):
            eight = pl.ds(pl.multiple_of(tile * 8, 8), 8)

            def value(k):
                start = pl.multiple_of(tile * 8 * own_m, 8) + k % own_m
                return flat[k // own_m, pl.ds(start, 8, stride=own_m), :]

            for one in range(0, count, group):
                left = [value(one + i) for i in range(group)]
                for other in range(one, count, group):
                    right = left if other == one else [value(other + i) for i in range(group)]
                    up = [None] * group
                    down = [None] * group
                    for i in range(group):
                        for j in range(i + 1 if other == one else 0, group):
                            above = jnp.where(left[i] > right[j], 1.0, 0.0)
                            up[i] = above if up[i] is None else up[i] + above
                            down[j] = above if down[j] is None else down[j] + above
                    for i in range(group):
                        if other == one:
                            less = float(i)
                            if up[i] is not None:
                                less = less + up[i]
                            if down[i] is not None:
                                less = less - down[i]
                            grads[one + i, eight, :] = less if one == 0 else grads[one + i, eight, :] + less
                        else:
                            grads[one + i, eight, :] += up[i]
                            below = float(group) - down[i]
                            grads[other + i, eight, :] = below if one == 0 else grads[other + i, eight, :] + below
            target = tgt[channel_half, eight, at]
            for k in range(count):
                grad = jnp.where(value(k) > target, float(2 * (count - 1)), 0.0) - 2.0 * grads[k, eight, :]
                grads[k, eight, :] = grad * area_row
            return 0

        lax.fori_loop(0, HALF_ROWS // 8, rank_rows, 0)

        def pack(k, _):
            back[chunk, k] = grads[k].astype(BF16)
            return 0

        lax.fori_loop(0, count, pack, 0)
        for k in range(1, members_n):
            grads_to(k, chunk).start()
        own_grads(chunk).start()

    def grads_place(chunk):
        channel_half, at = place(me, chunk)
        return og.at[:, pl.ds(pl.multiple_of(channel_half * HALF_ROWS, HALF_ROWS), HALF_ROWS), at]

    def grads_to(k, chunk):
        peer = member_peer(k)
        return pltpu.make_async_remote_copy(
            src_ref=back.at[chunk, pl.ds(peer * own_m, own_m)],
            dst_ref=grads_place(chunk),
            send_sem=back_send.at[chunk],
            recv_sem=back_recv.at[chunk],
            device_id={"member": peer},
            device_id_type=MESH,
        )

    def own_grads(chunk):
        return pltpu.make_async_copy(
            back.at[chunk, pl.ds(me * own_m, own_m)], grads_place(chunk), back_own.at[chunk]
        )

    def wait_grads(chunk):
        own_grads(chunk).wait()
        rest = back.at[chunk, 0 : count - own_m]
        pltpu.make_async_copy(rest, rest, back_recv.at[chunk]).wait()

    rank(0)

    pair_w.wait_recv()

    def weights():
        return wall[...].reshape(hid, wide + LANES)

    wt[...] = weights()[:, 0:wide].T

    nb = min(512, half_cells)

    def forward(chunk):
        def step(m, _):
            for b in range(0, half_cells, nb):
                at = slice(chunk * half_cells + b, chunk * half_cells + b + nb)
                bias2 = jnp.concatenate([bias_b[...]] * (nb // LANES), axis=1)
                v = dot_nn(wt[...], x[m, :, at]) + bias2
                sq = v * v
                u = 0.5 + 0.5 * jnp.tanh(v * (ROOT + (ROOT * CUBIC) * sq))
                a = v * u
                act[m, :, at] = a.astype(BF16)
                slope[m, :, at] = (u + a * (1.0 - u) * (2.0 * ROOT + (6.0 * ROOT * CUBIC) * sq)).astype(BF16)
            return 0

        lax.fori_loop(0, own_m, step, 0)

    for load in loads:
        load.wait()
    forward(0)
    forward(1)
    rank(1)

    def cut(chunk):
        return slice(chunk * half_cells, (chunk + 1) * half_cells)

    def pre_grads(chunk):
        at = cut(chunk)
        wop = weights()[:, wide:]

        def step(m, _):
            p = dot_nn(wop, og[m, :, at]) * slope[m, :, at].astype(F32)
            pg[m, :, at] = p.astype(BF16)
            folded = p[:, 0:LANES]
            for c in range(1, half_cells // LANES):
                folded = folded + p[:, c * LANES : (c + 1) * LANES]
            acc_b[...] += folded
            return 0

        lax.fori_loop(0, own_m, step, 0)

    def weight_terms(chunk, of):
        at = cut(chunk)

        def step(m, _):
            acc_in[of, :] += dot_nt(x[m, of, at], pg[m, :, at])
            acc_out[of, :] += dot_nt(act[m, of, at], og[m, :, at])
            return 0

        lax.fori_loop(0, own_m, step, 0)

    def input_grads(chunk):
        at = cut(chunk)

        def step(m, _):
            ig[m, :, at] = dot_nn(weights()[:, 0:wide], pg[m, :, at]).astype(BF16)
            return 0

        lax.fori_loop(0, own_m, step, 0)

    mine = pl.ds(pl.multiple_of(my_half * half_hid, half_hid), half_hid)
    theirs = pl.ds(pl.multiple_of((1 - my_half) * half_hid, half_hid), half_hid)

    wait_grads(0)
    pre_grads(0)
    weight_terms(0, slice(0, hid))
    input_grads(0)
    wait_grads(1)
    pre_grads(1)
    weight_terms(1, theirs)

    last_lane = lax.broadcasted_iota(jnp.int32, (half_hid, LANES), 1) == LANES - 1

    def out_terms(of):
        return jnp.where(last_lane, jnp.sum(acc_b[of, :], axis=1, keepdims=True), acc_out[of, :])

    part[:, 0:wide] = acc_in[theirs, :].astype(BF16)
    part[:, wide:] = out_terms(theirs).astype(BF16)
    to_sibling = pltpu.make_async_remote_copy(
        src_ref=part, dst_ref=pair, send_sem=pair_sem.at[0], recv_sem=pair_sem.at[1],
        device_id={"member": sibling}, device_id_type=MESH,
    )
    to_sibling.start()
    weight_terms(1, mine)
    to_sibling.wait_recv()
    total[:, 0:wide] = (acc_in[mine, :] + pair[:, 0:wide].astype(F32)).astype(BF16)
    total[:, wide:] = (out_terms(mine) + pair[:, wide:].astype(F32)).astype(BF16)

    slot = lax.rem(here, half_spaces)

    def send_block(k, _):
        block = lax.rem(here + k, half_spaces)
        pltpu.make_async_remote_copy(
            src_ref=total.at[pl.ds(pl.multiple_of(block * rows, rows), rows), :],
            dst_ref=shares.at[slot],
            send_sem=red_send, recv_sem=red_recv,
            device_id={"space": space_peer(k)}, device_id_type=MESH,
        ).start()
        return 0

    lax.fori_loop(first, half_spaces, send_block, 0)

    @pl.when(core == 0)
    def _():
        pltpu.make_async_copy(
            total.at[pl.ds(pl.multiple_of(slot * rows, rows), rows), :], shares.at[slot], red_recv
        ).start()

    input_grads(1)

    pltpu.make_async_copy(shares, shares, red_recv).wait()
    value = shares[0].astype(F32)
    for k in range(1, half_spaces):
        value = value + shares[k].astype(F32)
    owned[me] = value.astype(BF16)

    for k in range(1, members_n):
        pltpu.make_async_remote_copy(
            src_ref=owned.at[me], dst_ref=owned.at[me], send_sem=fin_send, recv_sem=fin_recv,
            device_id={"member": member_peer(k)}, device_id_type=MESH,
        ).start()
    rest = owned.at[0 : members_n - 1]
    pltpu.make_async_copy(rest, rest, fin_recv).wait()
    result = owned[0].astype(F32)
    for k in range(1, members_n):
        result = result + owned[k].astype(F32)
    result_out[...] = result * scale

    for chunk in range(2):
        rest = got.at[chunk, 0 : members_n - 1]
        pltpu.make_async_copy(rest, rest, a2a_send.at[chunk]).wait()
        rest = back.at[chunk, 0 : count - own_m]
        pltpu.make_async_copy(rest, rest, back_send.at[chunk]).wait()
    pair_w.wait_send()
    to_sibling.wait_send()
    rest = owned.at[0 : members_n - 1]
    pltpu.make_async_copy(rest, rest, fin_send).wait()

    def wait_sent(peers):
        rest = wall.at[0:peers]
        pltpu.make_async_copy(rest, rest, w_send.at[0]).wait()
        rest = shares.at[0:peers]
        pltpu.make_async_copy(rest, rest, red_send).wait()

    @pl.when(core == 0)
    def _():
        wait_sent(half_spaces - 1)

    @pl.when(core == 1)
    def _():
        wait_sent(half_spaces)


def body(members_n, spaces_n, inputs, w_in, bias_in, w_out, members_out, target, cell_area):
    own_m, hid, cells = inputs.shape
    rows, chan = w_out.shape
    wide = w_in.shape[1]
    count = own_m * members_n
    scale = 1.0 / math.sqrt(count * cells * spaces_n)
    half_chan = (chan + 1) // 2
    half_spaces = spaces_n // 2
    hbm_spec = pl.BlockSpec(memory_space=pltpu.HBM)
    vmem_spec = pl.BlockSpec(memory_space=pltpu.VMEM)
    dma = pltpu.SemaphoreType.DMA
    hidden = (own_m, hid, cells)
    full = wide + LANES
    operands = (
        inputs, w_in, bias_in.reshape(1, -1), w_out, members_out.transpose(1, 0, 2), target,
        cell_area.reshape(1, -1),
    )
    input_grad, result = pl.pallas_call(
        functools.partial(kernel, members_n, spaces_n, chan, scale),
        out_shape=(pltpu.VMEM(hidden, BF16), jax.ShapeDtypeStruct((rows, full), F32)),
        in_specs=[hbm_spec] * 7,
        out_specs=(vmem_spec, vmem_spec),
        scratch_shapes=[
            pltpu.VMEM(hidden, BF16),
            pltpu.VMEM((1, hid), F32),
            pltpu.VMEM((1, cells), F32),
            pltpu.VMEM((rows, full), BF16),
            pltpu.VMEM((rows, chan), BF16),
            pltpu.VMEM((rows, LANES), F32),
            pltpu.VMEM((spaces_n, rows, full), BF16),
            pltpu.VMEM((wide, hid), BF16),
            pltpu.VMEM((hid, LANES), F32),
            pltpu.VMEM((2, members_n, half_chan, own_m, LANES), F32),
            pltpu.VMEM((members_n, HALF_ROWS * own_m, LANES), F32),
            pltpu.VMEM((chan, cells), F32),
            pltpu.VMEM((2, HALF_ROWS, cells), F32),
            pltpu.VMEM((count, HALF_ROWS, LANES), F32),
            pltpu.VMEM((2, count, HALF_ROWS, LANES), BF16),
            pltpu.VMEM((own_m, LANES, cells), BF16),
            pltpu.VMEM(hidden, BF16),
            pltpu.VMEM(hidden, BF16),
            pltpu.VMEM(hidden, BF16),
            pltpu.VMEM((hid, wide), F32),
            pltpu.VMEM((hid, LANES), F32),
            pltpu.VMEM((hid, LANES), F32),
            pltpu.VMEM((hid // 2, full), BF16),
            pltpu.VMEM((hid // 2, full), BF16),
            pltpu.VMEM((hid // 2, full), BF16),
            pltpu.VMEM((half_spaces, rows, full), BF16),
            pltpu.VMEM((members_n, rows, full), BF16),
            dma((own_m + 5,)),
            dma((2,)),
            dma((2,)),
            dma((2,)),
            dma((2,)),
            dma((2,)),
            dma((2,)),
            dma((2,)),
            dma((2,)),
            dma((2,)),
            dma,
            dma,
            dma,
            dma,
        ],
        compiler_params=pltpu.CompilerParams(
            collective_id=0, has_side_effects=True, vmem_limit_bytes=48 * 1024 * 1024
        ),
        name="crps_backward",
    )(*(pltpu.with_memory_space_constraint(operand, pltpu.HBM) for operand in operands))
    second = wide + HALF_ROWS + 2 * half_chan - chan
    w_out_grad = jnp.concatenate(
        [result[:, wide : wide + half_chan], result[:, second : second + chan - half_chan]], axis=1
    )
    return input_grad, result[:, 0:wide], w_out_grad, result[:, full - 1]


def solution(mesh):
    members_n, spaces_n = mesh.shape["member"], mesh.shape["space"]
    return jax.shard_map(
        functools.partial(body, members_n, spaces_n),
        mesh=mesh,
        in_specs=(
            P("member", None, "space"),
            P("space", None),
            P(),
            P("space", None),
            P("member", None, "space"),
            P(None, "space"),
            P("space"),
        ),
        out_specs=(P("member", None, "space"), P("space", None), P("space", None), P("space")),
        check_vma=False,
    )
```

```python
import functools
import math

import jax
import jax.numpy as jnp
from jax import lax
from jax.experimental import pallas as pl
from jax.experimental.pallas import tpu as pltpu
from jax.sharding import PartitionSpec as P

CUBIC = 0.044715
ROOT = 0.7978845608028654
MESH = pl.DeviceIdType.MESH
F32 = jnp.float32
BF16 = jnp.bfloat16
LANES = 128
HALF_ROWS = 48


def dot_nn(a, b):
    return jnp.dot(a, b, preferred_element_type=F32)


def dot_nt(a, b):
    return lax.dot_general(a, b, (((1,), (1,)), ((), ())), preferred_element_type=F32)


def power(exponent):
    near = jnp.exp2(exponent)
    spread = near * float(2**16 + 1)
    return spread - (spread - near)


def kernel(
    members_n, spaces_n, chan,
    x_hbm, w_hbm, bias_hbm, wo_hbm, mem_hbm, tgt_hbm, area_hbm,
    ig, owned,
    x, bias_ref, area_ref, stage, wo_raw, wo_wide, wall, wt, bias_b, mem, flat, packed, got, values,
    tgt_raw, tgt, grads, back, og, act, slope, pg, acc_in, acc_out, acc_b, part, pair, total, shares,
    load_sem, w_recv, w_send, a2a_recv, a2a_send, a2a_own, back_recv, back_send, back_own,
    pair_sem, red_recv, red_send, fin_recv, fin_send,
):
    me = lax.axis_index("member")
    here = lax.axis_index("space")
    core = lax.rem(me, 2)
    own_m, hid, cells = x.shape
    rows = w_hbm.shape[0]
    half_spaces = spaces_n // 2
    half_members = members_n // 2
    half_hid = hid // 2
    half_cells = cells // 2
    count = own_m * members_n
    wide = wt.shape[0]
    half_chan = (chan + 1) // 2
    words = own_m - 1
    my_half = lax.rem(here // half_spaces + core, 2)
    sibling = me + 1 - 2 * core

    def member_peer(k):
        return lax.rem(me + k, members_n)

    def space_peer(k):
        return my_half * half_spaces + lax.rem(here + k, half_spaces)

    barrier = pltpu.get_barrier_semaphore()

    def greet_space(k, _):
        pl.semaphore_signal(barrier, inc=1, device_id={"space": space_peer(k)}, device_id_type=MESH)
        return 0

    def greet_member(k, _):
        pl.semaphore_signal(barrier, inc=1, device_id={"member": member_peer(k)}, device_id_type=MESH)
        return 0

    first = 1 - core
    lax.fori_loop(first, half_spaces, greet_space, 0)
    lax.fori_loop(1, members_n, greet_member, 0)

    load_w = pltpu.make_async_copy(w_hbm, stage.at[:, 0:wide], load_sem.at[own_m])
    load_wo = pltpu.make_async_copy(wo_hbm, wo_raw, load_sem.at[own_m + 1])
    load_tgt = pltpu.make_async_copy(tgt_hbm, tgt_raw, load_sem.at[own_m + 2])
    load_bias = pltpu.make_async_copy(bias_hbm, bias_ref, load_sem.at[own_m + 3])
    load_area = pltpu.make_async_copy(area_hbm, area_ref, load_sem.at[own_m + 4])
    loads = [pltpu.make_async_copy(x_hbm.at[m], x.at[m], load_sem.at[m]) for m in range(own_m)]
    load_mem = [
        pltpu.make_async_copy(
            mem_hbm.at[:, :, t * LANES : (t + 1) * LANES], mem.at[t], load_sem.at[own_m + 5 + t]
        )
        for t in range(members_n)
    ]
    for load in load_mem:
        load.start()
    load_w.start()
    load_wo.start()
    load_tgt.start()
    load_bias.start()
    load_area.start()
    for load in loads:
        load.start()

    wo_wide[...] = jnp.zeros(wo_wide.shape, F32)
    load_wo.wait()
    wo_wide[:, 0:half_chan] = wo_raw[:, 0:half_chan].astype(F32)
    second = HALF_ROWS + 2 * half_chan - chan
    wo_wide[:, second : second + chan - half_chan] = wo_raw[:, half_chan:chan].astype(F32)
    stage[:, wide:] = wo_wide[...].astype(BF16)
    load_w.wait()

    def place(peer, chunk):
        channel_half = lax.rem(peer // half_members + chunk, 2)
        tile = lax.rem(peer, half_members) + chunk * half_members
        return channel_half, pl.ds(pl.multiple_of(tile * LANES, LANES), LANES)

    flat[half_chan * own_m :, :] = jnp.zeros((flat.shape[0] - half_chan * own_m, LANES), F32)

    def encode(chunk):
        def step(peer, _):
            channel_half, _ = place(peer, chunk)
            tile = lax.rem(peer, half_members) + chunk * half_members
            start = channel_half * (chan - half_chan)
            for c in range(half_chan):
                flat[c * own_m : (c + 1) * own_m, :] = mem[tile, start + c]
            for i in reversed(range(HALF_ROWS // 8)):
                whole = [
                    flat[pl.ds(i * 8 * own_m + m, 8, stride=own_m), :] * float(2**18) for m in range(own_m)
                ]
                code = whole[words] - float(2**21)
                size = jnp.abs(code)
                digit2 = jnp.floor(size * (1.0 / 2**14))
                size = size - digit2 * float(2**14)
                digit1 = jnp.floor(size * (1.0 / 2**7))
                digits = (size - digit1 * float(2**7), digit1, digit2)
                for j in range(words):
                    word = (whole[j] + float(2**23)) * power(digits[j] - 64.0)
                    if j == words - 1:
                        word = jnp.where(code < 0.0, -word, word)
                    packed[chunk, peer, j * half_chan + i * 8 : j * half_chan + (i + 1) * 8, :] = word
            return 0

        lax.fori_loop(0, members_n, step, 0)

    def decode(chunk):
        def step(source, _):
            for i in range(HALF_ROWS // 8):
                rank_rows = slice(i * 8, (i + 1) * 8)
                digits = [None] * words
                for j in range(words):
                    word = got[chunk, source, j * half_chan + i * 8 : j * half_chan + (i + 1) * 8, :]
                    size = jnp.abs(word) if j == words - 1 else word
                    digits[j] = jnp.floor(jnp.log2(size) + 0.2) + (64.0 - 23.0)
                    values[source * own_m + j, rank_rows, :] = size * power(64.0 - digits[j]) - float(2**23)
                code = (digits[2] * 128.0 + digits[1]) * 128.0 + digits[0]
                values[source * own_m + words, rank_rows, :] = jnp.where(word < 0.0, -code, code) + float(2**21)
            return 0

        lax.fori_loop(0, members_n, step, 0)

    def values_to(k, chunk):
        peer = member_peer(k)
        return pltpu.make_async_remote_copy(
            src_ref=packed.at[chunk, peer],
            dst_ref=got.at[chunk, me],
            send_sem=a2a_send.at[chunk],
            recv_sem=a2a_recv.at[chunk],
            device_id={"member": peer},
            device_id_type=MESH,
        )

    def own_values(chunk):
        return pltpu.make_async_copy(packed.at[chunk, me], got.at[chunk, me], a2a_own.at[chunk])

    def send_values(chunk):
        for k in range(1, members_n):
            values_to(k, chunk).start()
        own_values(chunk).start()

    def values_sent(chunk):
        rest = got.at[chunk, 0 : members_n - 1]
        pltpu.make_async_copy(rest, rest, a2a_send.at[chunk]).wait()

    def send_rows(k, _):
        pltpu.make_async_remote_copy(
            src_ref=stage, dst_ref=wall.at[here], send_sem=w_send.at[0], recv_sem=w_recv.at[0],
            device_id={"space": space_peer(k)}, device_id_type=MESH,
        ).start()
        return 0

    for load in load_mem:
        load.wait()
    encode(0)
    encode(1)
    pl.semaphore_wait(barrier, members_n - 1 + half_spaces - first)
    send_values(0)
    lax.fori_loop(first, half_spaces, send_rows, 0)

    @pl.when(core == 0)
    def _():
        pltpu.make_async_copy(stage, wall.at[here], w_recv.at[0]).start()

    send_values(1)

    load_bias.wait()
    load_area.wait()
    bias_b[...] = jnp.broadcast_to(bias_ref[...], (LANES, hid)).T
    og[:, 2 * HALF_ROWS :, :] = jnp.zeros((own_m, og.shape[1] - 2 * HALF_ROWS, cells), BF16)
    tgt[...] = jnp.zeros(tgt.shape, F32)
    acc_in[...] = jnp.zeros(acc_in.shape, F32)
    acc_out[...] = jnp.zeros(acc_out.shape, F32)
    acc_b[...] = jnp.zeros(acc_b.shape, F32)
    load_tgt.wait()
    tgt[0, 0:half_chan, :] = tgt_raw[0:half_chan, :] * float(2**18)
    tgt[1, 0:half_chan, :] = tgt_raw[chan - half_chan : chan, :] * float(2**18)

    mine_w = wall.at[pl.ds(my_half * half_spaces, half_spaces)]
    pltpu.make_async_copy(mine_w, mine_w, w_recv.at[0]).wait()
    pair_w = pltpu.make_async_remote_copy(
        src_ref=mine_w, dst_ref=mine_w, send_sem=w_send.at[1], recv_sem=w_recv.at[1],
        device_id={"member": sibling}, device_id_type=MESH,
    )
    pair_w.start()

    group = 8

    def rank(chunk):
        own_values(chunk).wait()
        rest = got.at[chunk, 0 : members_n - 1]
        pltpu.make_async_copy(rest, rest, a2a_recv.at[chunk]).wait()
        channel_half, at = place(me, chunk)
        area_row = area_ref[:, at] * (1.0 / count)

        decode(chunk)

        def rank_rows(tile, _):
            eight = pl.ds(pl.multiple_of(tile * 8, 8), 8)

            def value(k):
                return values[k, eight, :]

            for one in range(0, count, group):
                left = [value(one + i) for i in range(group)]
                for other in range(one, count, group):
                    right = left if other == one else [value(other + i) for i in range(group)]
                    up = [None] * group
                    down = [None] * group
                    for i in range(group):
                        for j in range(i + 1 if other == one else 0, group):
                            above = jnp.where(left[i] > right[j], 1.0, 0.0)
                            up[i] = above if up[i] is None else up[i] + above
                            down[j] = above if down[j] is None else down[j] + above
                    for i in range(group):
                        if other == one:
                            less = float(i)
                            if up[i] is not None:
                                less = less + up[i]
                            if down[i] is not None:
                                less = less - down[i]
                            grads[one + i, eight, :] = less if one == 0 else grads[one + i, eight, :] + less
                        else:
                            grads[one + i, eight, :] += up[i]
                            below = float(group) - down[i]
                            grads[other + i, eight, :] = below if one == 0 else grads[other + i, eight, :] + below
            target = tgt[channel_half, eight, at]
            for k in range(count):
                grad = jnp.where(value(k) > target, float(2 * (count - 1)), 0.0) - 2.0 * grads[k, eight, :]
                grads[k, eight, :] = grad * area_row
            return 0

        lax.fori_loop(0, HALF_ROWS // 8, rank_rows, 0)

        def pack(k, _):
            back[chunk, k] = grads[k].astype(BF16)
            return 0

        lax.fori_loop(0, count, pack, 0)

    def send_grads(chunk):
        for k in range(1, members_n):
            grads_to(k, chunk).start()
        own_grads(chunk).start()

    def grads_place(chunk):
        channel_half, at = place(me, chunk)
        return og.at[:, pl.ds(pl.multiple_of(channel_half * HALF_ROWS, HALF_ROWS), HALF_ROWS), at]

    def grads_to(k, chunk):
        peer = member_peer(k)
        return pltpu.make_async_remote_copy(
            src_ref=back.at[chunk, pl.ds(peer * own_m, own_m)],
            dst_ref=grads_place(chunk),
            send_sem=back_send.at[chunk],
            recv_sem=back_recv.at[chunk],
            device_id={"member": peer},
            device_id_type=MESH,
        )

    def own_grads(chunk):
        return pltpu.make_async_copy(
            back.at[chunk, pl.ds(me * own_m, own_m)], grads_place(chunk), back_own.at[chunk]
        )

    def wait_grads(chunk):
        own_grads(chunk).wait()
        rest = back.at[chunk, 0 : count - own_m]
        pltpu.make_async_copy(rest, rest, back_recv.at[chunk]).wait()

    rank(0)
    values_sent(1)
    send_grads(0)

    pair_w.wait_recv()

    def weights():
        return wall[...].reshape(hid, wide + LANES)

    wt[...] = weights()[:, 0:wide].T

    nb = min(512, half_cells)

    def forward(chunk):
        def step(m, _):
            for b in range(0, half_cells, nb):
                at = slice(chunk * half_cells + b, chunk * half_cells + b + nb)
                bias2 = jnp.concatenate([bias_b[...]] * (nb // LANES), axis=1)
                v = dot_nn(wt[...], x[m, :, at]) + bias2
                sq = v * v
                u = 0.5 + 0.5 * jnp.tanh(v * (ROOT + (ROOT * CUBIC) * sq))
                a = v * u
                act[m, :, at] = a.astype(BF16)
                slope[m, :, at] = (u + a * (1.0 - u) * (2.0 * ROOT + (6.0 * ROOT * CUBIC) * sq)).astype(BF16)
            return 0

        lax.fori_loop(0, own_m, step, 0)

    for load in loads:
        load.wait()
    forward(0)
    rank(1)
    send_grads(1)
    forward(1)

    def cut(chunk):
        return slice(chunk * half_cells, (chunk + 1) * half_cells)

    def pre_grads(chunk):
        at = cut(chunk)
        wop = weights()[:, wide:]

        def step(m, _):
            p = dot_nn(wop, og[m, :, at]) * slope[m, :, at].astype(F32)
            pg[m, :, at] = p.astype(BF16)
            folded = p[:, 0:LANES]
            for c in range(1, half_cells // LANES):
                folded = folded + p[:, c * LANES : (c + 1) * LANES]
            acc_b[...] += folded
            return 0

        lax.fori_loop(0, own_m, step, 0)

    def weight_terms(chunk, of):
        at = cut(chunk)

        def step(m, _):
            acc_in[of, :] += dot_nt(x[m, of, at], pg[m, :, at])
            acc_out[of, :] += dot_nt(act[m, of, at], og[m, :, at])
            return 0

        lax.fori_loop(0, own_m, step, 0)

    def input_grads(chunk):
        at = cut(chunk)

        def step(m, _):
            ig[m, :, at] = dot_nn(weights()[:, 0:wide], pg[m, :, at]).astype(BF16)
            return 0

        lax.fori_loop(0, own_m, step, 0)

    mine = pl.ds(pl.multiple_of(my_half * half_hid, half_hid), half_hid)
    theirs = pl.ds(pl.multiple_of((1 - my_half) * half_hid, half_hid), half_hid)

    wait_grads(0)
    pre_grads(0)
    weight_terms(0, slice(0, hid))
    wait_grads(1)
    pre_grads(1)
    weight_terms(1, theirs)

    last_lane = lax.broadcasted_iota(jnp.int32, (half_hid, LANES), 1) == LANES - 1

    def out_terms(of):
        return jnp.where(last_lane, jnp.sum(acc_b[of, :], axis=1, keepdims=True), acc_out[of, :])

    part[:, 0:wide] = acc_in[theirs, :].astype(BF16)
    part[:, wide:] = out_terms(theirs).astype(BF16)
    to_sibling = pltpu.make_async_remote_copy(
        src_ref=part, dst_ref=pair, send_sem=pair_sem.at[0], recv_sem=pair_sem.at[1],
        device_id={"member": sibling}, device_id_type=MESH,
    )
    to_sibling.start()
    weight_terms(1, mine)
    to_sibling.wait_recv()
    total[:, 0:wide] = (acc_in[mine, :] + pair[:, 0:wide].astype(F32)).astype(BF16)
    total[:, wide:] = (out_terms(mine) + pair[:, wide:].astype(F32)).astype(BF16)

    slot = lax.rem(here, half_spaces)

    def send_block(k, _):
        block = lax.rem(here + k, half_spaces)
        pltpu.make_async_remote_copy(
            src_ref=total.at[pl.ds(pl.multiple_of(block * rows, rows), rows), :],
            dst_ref=shares.at[slot],
            send_sem=red_send, recv_sem=red_recv,
            device_id={"space": space_peer(k)}, device_id_type=MESH,
        ).start()
        return 0

    lax.fori_loop(first, half_spaces, send_block, 0)

    @pl.when(core == 0)
    def _():
        pltpu.make_async_copy(
            total.at[pl.ds(pl.multiple_of(slot * rows, rows), rows), :], shares.at[slot], red_recv
        ).start()

    input_grads(0)
    input_grads(1)

    pltpu.make_async_copy(shares, shares, red_recv).wait()
    value = shares[0].astype(F32)
    for k in range(1, half_spaces):
        value = value + shares[k].astype(F32)
    owned[me] = value.astype(BF16)

    for k in range(1, members_n):
        pltpu.make_async_remote_copy(
            src_ref=owned.at[me], dst_ref=owned.at[me], send_sem=fin_send, recv_sem=fin_recv,
            device_id={"member": member_peer(k)}, device_id_type=MESH,
        ).start()
    rest = owned.at[0 : members_n - 1]
    pltpu.make_async_copy(rest, rest, fin_recv).wait()
    values_sent(0)
    for chunk in range(2):
        rest = back.at[chunk, 0 : count - own_m]
        pltpu.make_async_copy(rest, rest, back_send.at[chunk]).wait()
    pair_w.wait_send()
    to_sibling.wait_send()
    rest = owned.at[0 : members_n - 1]
    pltpu.make_async_copy(rest, rest, fin_send).wait()

    def wait_sent(peers):
        rest = wall.at[0:peers]
        pltpu.make_async_copy(rest, rest, w_send.at[0]).wait()
        rest = shares.at[0:peers]
        pltpu.make_async_copy(rest, rest, red_send).wait()

    @pl.when(core == 0)
    def _():
        wait_sent(half_spaces - 1)

    @pl.when(core == 1)
    def _():
        wait_sent(half_spaces)


def finish(
    chan, scale, ig_ref, owned_ref, ig_out, win_out, wout_out, bias_out, win, wout, bias, sem
):
    copies = [pltpu.make_async_copy(ig_ref.at[m], ig_out.at[m], sem.at[m]) for m in range(ig_ref.shape[0])]
    for copy in copies:
        copy.start()
    members_n, rows, full = owned_ref.shape
    wide = full - LANES
    half_chan = (chan + 1) // 2
    result = owned_ref[0].astype(F32)
    for k in range(1, members_n):
        result = result + owned_ref[k].astype(F32)
    result = result * scale
    win[...] = result[:, 0:wide]
    wout[:, 0:half_chan] = result[:, wide : wide + half_chan]
    second = wide + HALF_ROWS + 2 * half_chan - chan
    wout[:, half_chan:chan] = result[:, second : second + chan - half_chan]
    diagonal = lax.broadcasted_iota(jnp.int32, (rows, rows), 0) == lax.broadcasted_iota(
        jnp.int32, (rows, rows), 1
    )
    bias[...] = jnp.sum(jnp.where(diagonal, result[:, full - 1 : full], 0.0), axis=0, keepdims=True)
    first = len(copies)
    for k, (source, out) in enumerate(((win, win_out), (wout, wout_out), (bias, bias_out))):
        copies.append(pltpu.make_async_copy(source, out, sem.at[first + k]))
        copies[-1].start()
    for copy in copies:
        copy.wait()


def body(members_n, spaces_n, inputs, w_in, bias_in, w_out, members_out, target, cell_area):
    own_m, hid, cells = inputs.shape
    rows, chan = w_out.shape
    wide = w_in.shape[1]
    count = own_m * members_n
    scale = 1.0 / math.sqrt(count * cells * spaces_n)
    half_chan = (chan + 1) // 2
    packed_rows = (own_m - 2) * half_chan + HALF_ROWS
    half_spaces = spaces_n // 2
    hbm_spec = pl.BlockSpec(memory_space=pltpu.HBM)
    vmem_spec = pl.BlockSpec(memory_space=pltpu.VMEM)
    dma = pltpu.SemaphoreType.DMA
    hidden = (own_m, hid, cells)
    full = wide + LANES
    operands = (
        inputs, w_in, bias_in.reshape(1, -1), w_out, members_out.transpose(1, 0, 2), target,
        cell_area.reshape(1, -1),
    )
    partial = pl.pallas_call(
        functools.partial(kernel, members_n, spaces_n, chan),
        out_shape=(pltpu.VMEM(hidden, BF16), pltpu.VMEM((members_n, rows, full), BF16)),
        in_specs=[hbm_spec] * 7,
        out_specs=(vmem_spec, vmem_spec),
        scratch_shapes=[
            pltpu.VMEM(hidden, BF16),
            pltpu.VMEM((1, hid), F32),
            pltpu.VMEM((1, cells), F32),
            pltpu.VMEM((rows, full), BF16),
            pltpu.VMEM((rows, chan), BF16),
            pltpu.VMEM((rows, LANES), F32),
            pltpu.VMEM((spaces_n, rows, full), BF16),
            pltpu.VMEM((wide, hid), BF16),
            pltpu.VMEM((hid, LANES), F32),
            pltpu.VMEM((members_n, chan, own_m, LANES), F32),
            pltpu.VMEM((HALF_ROWS * own_m, LANES), F32),
            pltpu.VMEM((2, members_n, packed_rows, LANES), F32),
            pltpu.VMEM((2, members_n, packed_rows, LANES), F32),
            pltpu.VMEM((count, HALF_ROWS, LANES), F32),
            pltpu.VMEM((chan, cells), F32),
            pltpu.VMEM((2, HALF_ROWS, cells), F32),
            pltpu.VMEM((count, HALF_ROWS, LANES), F32),
            pltpu.VMEM((2, count, HALF_ROWS, LANES), BF16),
            pltpu.VMEM((own_m, LANES, cells), BF16),
            pltpu.VMEM(hidden, BF16),
            pltpu.VMEM(hidden, BF16),
            pltpu.VMEM(hidden, BF16),
            pltpu.VMEM((hid, wide), F32),
            pltpu.VMEM((hid, LANES), F32),
            pltpu.VMEM((hid, LANES), F32),
            pltpu.VMEM((hid // 2, full), BF16),
            pltpu.VMEM((hid // 2, full), BF16),
            pltpu.VMEM((hid // 2, full), BF16),
            pltpu.VMEM((half_spaces, rows, full), BF16),
            dma((own_m + 5 + members_n,)),
            dma((2,)),
            dma((2,)),
            dma((2,)),
            dma((2,)),
            dma((2,)),
            dma((2,)),
            dma((2,)),
            dma((2,)),
            dma((2,)),
            dma,
            dma,
            dma,
            dma,
        ],
        compiler_params=pltpu.CompilerParams(
            collective_id=0, has_side_effects=True, vmem_limit_bytes=48 * 1024 * 1024
        ),
        name="crps_backward",
    )(*(pltpu.with_memory_space_constraint(operand, pltpu.HBM) for operand in operands))
    input_grad, w_in_grad, w_out_grad, bias_grad = pl.pallas_call(
        functools.partial(finish, chan, scale),
        out_shape=(
            jax.ShapeDtypeStruct(hidden, BF16),
            jax.ShapeDtypeStruct((rows, wide), F32),
            jax.ShapeDtypeStruct((rows, chan), F32),
            jax.ShapeDtypeStruct((1, rows), F32),
        ),
        in_specs=[vmem_spec, vmem_spec],
        out_specs=(hbm_spec,) * 4,
        scratch_shapes=[
            pltpu.VMEM((rows, wide), F32),
            pltpu.VMEM((rows, chan), F32),
            pltpu.VMEM((1, rows), F32),
            dma((own_m + 3,)),
        ],
        compiler_params=pltpu.CompilerParams(vmem_limit_bytes=16 * 1024 * 1024),
        name="finish",
    )(*(pltpu.with_memory_space_constraint(array, pltpu.VMEM) for array in partial))
    return input_grad, w_in_grad, w_out_grad, bias_grad.reshape(rows)


def solution(mesh):
    members_n, spaces_n = mesh.shape["member"], mesh.shape["space"]
    return jax.shard_map(
        functools.partial(body, members_n, spaces_n),
        mesh=mesh,
        in_specs=(
            P("member", None, "space"),
            P("space", None),
            P(),
            P("space", None),
            P("member", None, "space"),
            P(None, "space"),
            P("space"),
        ),
        out_specs=(P("member", None, "space"), P("space", None), P("space", None), P("space")),
        check_vma=False,
    )
```

```python
import functools
import math

import jax
import jax.numpy as jnp
from jax import lax
from jax.experimental import pallas as pl
from jax.experimental.pallas import tpu as pltpu
from jax.sharding import PartitionSpec as P

CUBIC = 0.044715
ROOT = 0.7978845608028654
MESH = pl.DeviceIdType.MESH
F32 = jnp.float32
BF16 = jnp.bfloat16
LANES = 128
HALF_ROWS = 48


def dot_nn(a, b):
    return jnp.dot(a, b, preferred_element_type=F32)


def dot_nt(a, b):
    return lax.dot_general(a, b, (((1,), (1,)), ((), ())), preferred_element_type=F32)


def power(exponent):
    near = jnp.exp2(exponent)
    spread = near * float(2**16 + 1)
    return spread - (spread - near)


def kernel(
    members_n, spaces_n, chan,
    x_hbm, w_hbm, bias_hbm, wo_hbm, mem_hbm, tgt_hbm, area_hbm,
    ig, owned,
    x, bias_ref, area_ref, stage, wo_raw, wo_wide, wall, wt, bias_b, mem, flat, packed, got, values,
    tgt_raw, tgt, grads, back, og, act, slope, pg, acc_in, acc_out, acc_b, part, pair, total, shares,
    load_sem, w_recv, w_send, a2a_recv, a2a_send, a2a_own, back_recv, back_send, back_own,
    pair_sem, red_recv, red_send, fin_recv, fin_send,
):
    me = lax.axis_index("member")
    here = lax.axis_index("space")
    core = lax.rem(me, 2)
    own_m, hid, cells = x.shape
    rows = w_hbm.shape[0]
    half_spaces = spaces_n // 2
    half_members = members_n // 2
    half_hid = hid // 2
    half_cells = cells // 2
    count = own_m * members_n
    wide = wt.shape[0]
    half_chan = (chan + 1) // 2
    words = own_m - 1
    my_half = lax.rem(here // half_spaces + core, 2)
    sibling = me + 1 - 2 * core

    def member_peer(k):
        return lax.rem(me + k, members_n)

    def space_peer(k):
        return my_half * half_spaces + lax.rem(here + k, half_spaces)

    far_first = sorted(range(1, members_n), key=lambda k: -min(k, members_n - k))
    barrier = pltpu.get_barrier_semaphore()

    def greet_space(k, _):
        pl.semaphore_signal(barrier, inc=1, device_id={"space": space_peer(k)}, device_id_type=MESH)
        return 0

    def greet_member(k, _):
        pl.semaphore_signal(barrier, inc=1, device_id={"member": member_peer(k)}, device_id_type=MESH)
        return 0

    first = 1 - core
    lax.fori_loop(first, half_spaces, greet_space, 0)
    lax.fori_loop(1, members_n, greet_member, 0)

    load_w = pltpu.make_async_copy(w_hbm, stage.at[:, 0:wide], load_sem.at[own_m])
    load_wo = pltpu.make_async_copy(wo_hbm, wo_raw, load_sem.at[own_m + 1])
    load_tgt = pltpu.make_async_copy(tgt_hbm, tgt_raw, load_sem.at[own_m + 2])
    load_bias = pltpu.make_async_copy(bias_hbm, bias_ref, load_sem.at[own_m + 3])
    load_area = pltpu.make_async_copy(area_hbm, area_ref, load_sem.at[own_m + 4])
    loads = [pltpu.make_async_copy(x_hbm.at[m], x.at[m], load_sem.at[m]) for m in range(own_m)]
    load_mem = [
        pltpu.make_async_copy(
            mem_hbm.at[:, :, t * LANES : (t + 1) * LANES], mem.at[t], load_sem.at[own_m + 5 + t]
        )
        for t in range(members_n)
    ]
    for load in load_mem:
        load.start()
    load_w.start()
    load_wo.start()
    load_tgt.start()
    load_bias.start()
    load_area.start()
    for load in loads:
        load.start()

    wo_wide[...] = jnp.zeros(wo_wide.shape, F32)
    load_wo.wait()
    wo_wide[:, 0:half_chan] = wo_raw[:, 0:half_chan].astype(F32)
    second = HALF_ROWS + 2 * half_chan - chan
    wo_wide[:, second : second + chan - half_chan] = wo_raw[:, half_chan:chan].astype(F32)
    stage[:, wide:] = wo_wide[...].astype(BF16)
    load_w.wait()

    def place(peer, chunk):
        channel_half = lax.rem(peer // half_members + chunk, 2)
        tile = lax.rem(peer, half_members) + chunk * half_members
        return channel_half, pl.ds(pl.multiple_of(tile * LANES, LANES), LANES)

    flat[half_chan * own_m :, :] = jnp.zeros((flat.shape[0] - half_chan * own_m, LANES), F32)

    def encode(chunk):
        def step(peer, _):
            channel_half, _ = place(peer, chunk)
            tile = lax.rem(peer, half_members) + chunk * half_members
            start = channel_half * (chan - half_chan)
            for c in range(half_chan):
                flat[c * own_m : (c + 1) * own_m, :] = mem[tile, start + c]
            for i in reversed(range(HALF_ROWS // 8)):
                whole = [
                    flat[pl.ds(i * 8 * own_m + m, 8, stride=own_m), :] * float(2**18) for m in range(own_m)
                ]
                code = whole[words] - float(2**21)
                size = jnp.abs(code)
                digit2 = jnp.floor(size * (1.0 / 2**14))
                size = size - digit2 * float(2**14)
                digit1 = jnp.floor(size * (1.0 / 2**7))
                digits = (size - digit1 * float(2**7), digit1, digit2)
                for j in range(words):
                    word = (whole[j] + float(2**23)) * power(digits[j] - 64.0)
                    if j == words - 1:
                        word = jnp.where(code < 0.0, -word, word)
                    packed[chunk, peer, j * half_chan + i * 8 : j * half_chan + (i + 1) * 8, :] = word
            return 0

        lax.fori_loop(0, members_n, step, 0)

    def decode(chunk):
        def step(source, _):
            for i in range(HALF_ROWS // 8):
                rank_rows = slice(i * 8, (i + 1) * 8)
                digits = [None] * words
                for j in range(words):
                    word = got[chunk, source, j * half_chan + i * 8 : j * half_chan + (i + 1) * 8, :]
                    size = jnp.abs(word) if j == words - 1 else word
                    digits[j] = jnp.floor(jnp.log2(size) + 0.2) + (64.0 - 23.0)
                    values[source * own_m + j, rank_rows, :] = size * power(64.0 - digits[j]) - float(2**23)
                code = (digits[2] * 128.0 + digits[1]) * 128.0 + digits[0]
                values[source * own_m + words, rank_rows, :] = jnp.where(word < 0.0, -code, code) + float(2**21)
            return 0

        lax.fori_loop(0, members_n, step, 0)

    def values_to(k, chunk):
        peer = member_peer(k)
        return pltpu.make_async_remote_copy(
            src_ref=packed.at[chunk, peer],
            dst_ref=got.at[chunk, me],
            send_sem=a2a_send.at[chunk],
            recv_sem=a2a_recv.at[chunk],
            device_id={"member": peer},
            device_id_type=MESH,
        )

    def own_values(chunk):
        return pltpu.make_async_copy(packed.at[chunk, me], got.at[chunk, me], a2a_own.at[chunk])

    def send_values(chunk):
        for k in far_first:
            values_to(k, chunk).start()
        own_values(chunk).start()

    def values_sent(chunk):
        rest = got.at[chunk, 0 : members_n - 1]
        pltpu.make_async_copy(rest, rest, a2a_send.at[chunk]).wait()

    def send_rows(k, _):
        pltpu.make_async_remote_copy(
            src_ref=stage, dst_ref=wall.at[here], send_sem=w_send.at[0], recv_sem=w_recv.at[0],
            device_id={"space": space_peer(k)}, device_id_type=MESH,
        ).start()
        return 0

    for load in load_mem:
        load.wait()
    encode(0)
    encode(1)
    pl.semaphore_wait(barrier, members_n - 1 + half_spaces - first)
    send_values(0)
    lax.fori_loop(first, half_spaces, send_rows, 0)

    @pl.when(core == 0)
    def _():
        pltpu.make_async_copy(stage, wall.at[here], w_recv.at[0]).start()

    send_values(1)

    load_bias.wait()
    load_area.wait()
    bias_b[...] = jnp.broadcast_to(bias_ref[...], (LANES, hid)).T
    og[:, 2 * HALF_ROWS :, :] = jnp.zeros((own_m, og.shape[1] - 2 * HALF_ROWS, cells), BF16)
    tgt[...] = jnp.zeros(tgt.shape, F32)
    acc_in[...] = jnp.zeros(acc_in.shape, F32)
    acc_out[...] = jnp.zeros(acc_out.shape, F32)
    acc_b[...] = jnp.zeros(acc_b.shape, F32)
    load_tgt.wait()
    tgt[0, 0:half_chan, :] = tgt_raw[0:half_chan, :] * float(2**18)
    tgt[1, 0:half_chan, :] = tgt_raw[chan - half_chan : chan, :] * float(2**18)

    mine_w = wall.at[pl.ds(my_half * half_spaces, half_spaces)]
    pltpu.make_async_copy(mine_w, mine_w, w_recv.at[0]).wait()
    pair_w = pltpu.make_async_remote_copy(
        src_ref=mine_w, dst_ref=mine_w, send_sem=w_send.at[1], recv_sem=w_recv.at[1],
        device_id={"member": sibling}, device_id_type=MESH,
    )
    pair_w.start()

    group = 8

    def rank(chunk):
        own_values(chunk).wait()
        rest = got.at[chunk, 0 : members_n - 1]
        pltpu.make_async_copy(rest, rest, a2a_recv.at[chunk]).wait()
        channel_half, at = place(me, chunk)
        area_row = area_ref[:, at] * (1.0 / count)

        decode(chunk)

        def rank_rows(tile, _):
            eight = pl.ds(pl.multiple_of(tile * 8, 8), 8)

            def value(k):
                return values[k, eight, :]

            for one in range(0, count, group):
                left = [value(one + i) for i in range(group)]
                for other in range(one, count, group):
                    right = left if other == one else [value(other + i) for i in range(group)]
                    up = [None] * group
                    down = [None] * group
                    for i in range(group):
                        for j in range(i + 1 if other == one else 0, group):
                            above = jnp.where(left[i] > right[j], 1.0, 0.0)
                            up[i] = above if up[i] is None else up[i] + above
                            down[j] = above if down[j] is None else down[j] + above
                    for i in range(group):
                        if other == one:
                            less = float(i)
                            if up[i] is not None:
                                less = less + up[i]
                            if down[i] is not None:
                                less = less - down[i]
                            grads[one + i, eight, :] = less if one == 0 else grads[one + i, eight, :] + less
                        else:
                            grads[one + i, eight, :] += up[i]
                            below = float(group) - down[i]
                            grads[other + i, eight, :] = below if one == 0 else grads[other + i, eight, :] + below
            target = tgt[channel_half, eight, at]
            for k in range(count):
                grad = jnp.where(value(k) > target, float(2 * (count - 1)), 0.0) - 2.0 * grads[k, eight, :]
                grads[k, eight, :] = grad * area_row
            return 0

        lax.fori_loop(0, HALF_ROWS // 8, rank_rows, 0)

        def pack(k, _):
            back[chunk, k] = grads[k].astype(BF16)
            return 0

        lax.fori_loop(0, count, pack, 0)

    def send_grads(chunk):
        for k in far_first:
            grads_to(k, chunk).start()
        own_grads(chunk).start()

    def grads_place(chunk):
        channel_half, at = place(me, chunk)
        return og.at[:, pl.ds(pl.multiple_of(channel_half * HALF_ROWS, HALF_ROWS), HALF_ROWS), at]

    def grads_to(k, chunk):
        peer = member_peer(k)
        return pltpu.make_async_remote_copy(
            src_ref=back.at[chunk, pl.ds(peer * own_m, own_m)],
            dst_ref=grads_place(chunk),
            send_sem=back_send.at[chunk],
            recv_sem=back_recv.at[chunk],
            device_id={"member": peer},
            device_id_type=MESH,
        )

    def own_grads(chunk):
        return pltpu.make_async_copy(
            back.at[chunk, pl.ds(me * own_m, own_m)], grads_place(chunk), back_own.at[chunk]
        )

    def wait_grads(chunk):
        own_grads(chunk).wait()
        rest = back.at[chunk, 0 : count - own_m]
        pltpu.make_async_copy(rest, rest, back_recv.at[chunk]).wait()

    rank(0)
    values_sent(1)
    send_grads(0)

    pair_w.wait_recv()

    def weights():
        return wall[...].reshape(hid, wide + LANES)

    wt[...] = weights()[:, 0:wide].T

    nb = min(512, half_cells)

    def forward(chunk):
        def step(m, _):
            for b in range(0, half_cells, nb):
                at = slice(chunk * half_cells + b, chunk * half_cells + b + nb)
                bias2 = jnp.concatenate([bias_b[...]] * (nb // LANES), axis=1)
                v = dot_nn(wt[...], x[m, :, at]) + bias2
                sq = v * v
                u = 0.5 + 0.5 * jnp.tanh(v * (ROOT + (ROOT * CUBIC) * sq))
                a = v * u
                act[m, :, at] = a.astype(BF16)
                slope[m, :, at] = (u + a * (1.0 - u) * (2.0 * ROOT + (6.0 * ROOT * CUBIC) * sq)).astype(BF16)
            return 0

        for m in range(own_m):
            step(m, 0)

    for load in loads:
        load.wait()
    forward(0)
    rank(1)
    send_grads(1)
    forward(1)

    def cut(chunk):
        return slice(chunk * half_cells, (chunk + 1) * half_cells)

    def pre_grads(chunk):
        at = cut(chunk)
        wop = weights()[:, wide:]

        def step(m, _):
            p = dot_nn(wop, og[m, :, at]) * slope[m, :, at].astype(F32)
            pg[m, :, at] = p.astype(BF16)
            folded = p[:, 0:LANES]
            for c in range(1, half_cells // LANES):
                folded = folded + p[:, c * LANES : (c + 1) * LANES]
            acc_b[...] += folded
            return 0

        for m in range(own_m):
            step(m, 0)

    def weight_terms(chunk, of):
        at = cut(chunk)
        acc_in[of, :] += functools.reduce(
            jnp.add, [dot_nt(x[m, of, at], pg[m, :, at]) for m in range(own_m)]
        )
        acc_out[of, :] += functools.reduce(
            jnp.add, [dot_nt(act[m, of, at], og[m, :, at]) for m in range(own_m)]
        )

    def input_grads(chunk):
        at = cut(chunk)

        def step(m, _):
            ig[m, :, at] = dot_nn(weights()[:, 0:wide], pg[m, :, at]).astype(BF16)
            return 0

        lax.fori_loop(0, own_m, step, 0)

    mine = pl.ds(pl.multiple_of(my_half * half_hid, half_hid), half_hid)
    theirs = pl.ds(pl.multiple_of((1 - my_half) * half_hid, half_hid), half_hid)

    wait_grads(0)
    pre_grads(0)
    weight_terms(0, slice(0, hid))
    wait_grads(1)
    pre_grads(1)
    weight_terms(1, theirs)

    last_lane = lax.broadcasted_iota(jnp.int32, (half_hid, LANES), 1) == LANES - 1

    def out_terms(of):
        return jnp.where(last_lane, jnp.sum(acc_b[of, :], axis=1, keepdims=True), acc_out[of, :])

    part[:, 0:wide] = acc_in[theirs, :].astype(BF16)
    part[:, wide:] = out_terms(theirs).astype(BF16)
    to_sibling = pltpu.make_async_remote_copy(
        src_ref=part, dst_ref=pair, send_sem=pair_sem.at[0], recv_sem=pair_sem.at[1],
        device_id={"member": sibling}, device_id_type=MESH,
    )
    to_sibling.start()
    weight_terms(1, mine)
    to_sibling.wait_recv()
    total[:, 0:wide] = (acc_in[mine, :] + pair[:, 0:wide].astype(F32)).astype(BF16)
    total[:, wide:] = (out_terms(mine) + pair[:, wide:].astype(F32)).astype(BF16)

    slot = lax.rem(here, half_spaces)

    def send_block(k, _):
        block = lax.rem(here + k, half_spaces)
        pltpu.make_async_remote_copy(
            src_ref=total.at[pl.ds(pl.multiple_of(block * rows, rows), rows), :],
            dst_ref=shares.at[slot],
            send_sem=red_send, recv_sem=red_recv,
            device_id={"space": space_peer(k)}, device_id_type=MESH,
        ).start()
        return 0

    lax.fori_loop(first, half_spaces, send_block, 0)

    @pl.when(core == 0)
    def _():
        pltpu.make_async_copy(
            total.at[pl.ds(pl.multiple_of(slot * rows, rows), rows), :], shares.at[slot], red_recv
        ).start()

    input_grads(0)
    input_grads(1)

    pltpu.make_async_copy(shares, shares, red_recv).wait()
    value = shares[0].astype(F32)
    for k in range(1, half_spaces):
        value = value + shares[k].astype(F32)
    owned[me] = value.astype(BF16)

    for k in far_first:
        pltpu.make_async_remote_copy(
            src_ref=owned.at[me], dst_ref=owned.at[me], send_sem=fin_send, recv_sem=fin_recv,
            device_id={"member": member_peer(k)}, device_id_type=MESH,
        ).start()
    rest = owned.at[0 : members_n - 1]
    pltpu.make_async_copy(rest, rest, fin_recv).wait()
    values_sent(0)
    for chunk in range(2):
        rest = back.at[chunk, 0 : count - own_m]
        pltpu.make_async_copy(rest, rest, back_send.at[chunk]).wait()
    pair_w.wait_send()
    to_sibling.wait_send()
    rest = owned.at[0 : members_n - 1]
    pltpu.make_async_copy(rest, rest, fin_send).wait()

    def wait_sent(peers):
        rest = wall.at[0:peers]
        pltpu.make_async_copy(rest, rest, w_send.at[0]).wait()
        rest = shares.at[0:peers]
        pltpu.make_async_copy(rest, rest, red_send).wait()

    @pl.when(core == 0)
    def _():
        wait_sent(half_spaces - 1)

    @pl.when(core == 1)
    def _():
        wait_sent(half_spaces)


def finish(
    chan, scale, ig_ref, owned_ref, ig_out, win_out, wout_out, bias_out, win, wout, bias, sem
):
    copies = [pltpu.make_async_copy(ig_ref.at[m], ig_out.at[m], sem.at[m]) for m in range(ig_ref.shape[0])]
    for copy in copies:
        copy.start()
    members_n, rows, full = owned_ref.shape
    wide = full - LANES
    half_chan = (chan + 1) // 2
    result = owned_ref[0].astype(F32)
    for k in range(1, members_n):
        result = result + owned_ref[k].astype(F32)
    result = result * scale
    win[...] = result[:, 0:wide]
    wout[:, 0:half_chan] = result[:, wide : wide + half_chan]
    second = wide + HALF_ROWS + 2 * half_chan - chan
    wout[:, half_chan:chan] = result[:, second : second + chan - half_chan]
    diagonal = lax.broadcasted_iota(jnp.int32, (rows, rows), 0) == lax.broadcasted_iota(
        jnp.int32, (rows, rows), 1
    )
    bias[...] = jnp.sum(jnp.where(diagonal, result[:, full - 1 : full], 0.0), axis=0, keepdims=True)
    first = len(copies)
    for k, (source, out) in enumerate(((win, win_out), (wout, wout_out), (bias, bias_out))):
        copies.append(pltpu.make_async_copy(source, out, sem.at[first + k]))
        copies[-1].start()
    for copy in copies:
        copy.wait()


def body(members_n, spaces_n, inputs, w_in, bias_in, w_out, members_out, target, cell_area):
    own_m, hid, cells = inputs.shape
    rows, chan = w_out.shape
    wide = w_in.shape[1]
    count = own_m * members_n
    scale = 1.0 / math.sqrt(count * cells * spaces_n)
    half_chan = (chan + 1) // 2
    packed_rows = (own_m - 2) * half_chan + HALF_ROWS
    half_spaces = spaces_n // 2
    hbm_spec = pl.BlockSpec(memory_space=pltpu.HBM)
    vmem_spec = pl.BlockSpec(memory_space=pltpu.VMEM)
    dma = pltpu.SemaphoreType.DMA
    hidden = (own_m, hid, cells)
    full = wide + LANES
    operands = (
        inputs, w_in, bias_in.reshape(1, -1), w_out, members_out.transpose(1, 0, 2), target,
        cell_area.reshape(1, -1),
    )
    partial = pl.pallas_call(
        functools.partial(kernel, members_n, spaces_n, chan),
        out_shape=(pltpu.VMEM(hidden, BF16), pltpu.VMEM((members_n, rows, full), BF16)),
        in_specs=[hbm_spec] * 7,
        out_specs=(vmem_spec, vmem_spec),
        scratch_shapes=[
            pltpu.VMEM(hidden, BF16),
            pltpu.VMEM((1, hid), F32),
            pltpu.VMEM((1, cells), F32),
            pltpu.VMEM((rows, full), BF16),
            pltpu.VMEM((rows, chan), BF16),
            pltpu.VMEM((rows, LANES), F32),
            pltpu.VMEM((spaces_n, rows, full), BF16),
            pltpu.VMEM((wide, hid), BF16),
            pltpu.VMEM((hid, LANES), F32),
            pltpu.VMEM((members_n, chan, own_m, LANES), F32),
            pltpu.VMEM((HALF_ROWS * own_m, LANES), F32),
            pltpu.VMEM((2, members_n, packed_rows, LANES), F32),
            pltpu.VMEM((2, members_n, packed_rows, LANES), F32),
            pltpu.VMEM((count, HALF_ROWS, LANES), F32),
            pltpu.VMEM((chan, cells), F32),
            pltpu.VMEM((2, HALF_ROWS, cells), F32),
            pltpu.VMEM((count, HALF_ROWS, LANES), F32),
            pltpu.VMEM((2, count, HALF_ROWS, LANES), BF16),
            pltpu.VMEM((own_m, LANES, cells), BF16),
            pltpu.VMEM(hidden, BF16),
            pltpu.VMEM(hidden, BF16),
            pltpu.VMEM(hidden, BF16),
            pltpu.VMEM((hid, wide), F32),
            pltpu.VMEM((hid, LANES), F32),
            pltpu.VMEM((hid, LANES), F32),
            pltpu.VMEM((hid // 2, full), BF16),
            pltpu.VMEM((hid // 2, full), BF16),
            pltpu.VMEM((hid // 2, full), BF16),
            pltpu.VMEM((half_spaces, rows, full), BF16),
            dma((own_m + 5 + members_n,)),
            dma((2,)),
            dma((2,)),
            dma((2,)),
            dma((2,)),
            dma((2,)),
            dma((2,)),
            dma((2,)),
            dma((2,)),
            dma((2,)),
            dma,
            dma,
            dma,
            dma,
        ],
        compiler_params=pltpu.CompilerParams(
            collective_id=0, has_side_effects=True, vmem_limit_bytes=48 * 1024 * 1024
        ),
        name="crps_backward",
    )(*(pltpu.with_memory_space_constraint(operand, pltpu.HBM) for operand in operands))
    input_grad, w_in_grad, w_out_grad, bias_grad = pl.pallas_call(
        functools.partial(finish, chan, scale),
        out_shape=(
            jax.ShapeDtypeStruct(hidden, BF16),
            jax.ShapeDtypeStruct((rows, wide), F32),
            jax.ShapeDtypeStruct((rows, chan), F32),
            jax.ShapeDtypeStruct((1, rows), F32),
        ),
        in_specs=[vmem_spec, vmem_spec],
        out_specs=(hbm_spec,) * 4,
        scratch_shapes=[
            pltpu.VMEM((rows, wide), F32),
            pltpu.VMEM((rows, chan), F32),
            pltpu.VMEM((1, rows), F32),
            dma((own_m + 3,)),
        ],
        compiler_params=pltpu.CompilerParams(vmem_limit_bytes=16 * 1024 * 1024),
        name="finish",
    )(*(pltpu.with_memory_space_constraint(array, pltpu.VMEM) for array in partial))
    return input_grad, w_in_grad, w_out_grad, bias_grad.reshape(rows)


def solution(mesh):
    members_n, spaces_n = mesh.shape["member"], mesh.shape["space"]
    return jax.shard_map(
        functools.partial(body, members_n, spaces_n),
        mesh=mesh,
        in_specs=(
            P("member", None, "space"),
            P("space", None),
            P(),
            P("space", None),
            P("member", None, "space"),
            P(None, "space"),
            P("space"),
        ),
        out_specs=(P("member", None, "space"), P("space", None), P("space", None), P("space")),
        check_vma=False,
    )
```

```python
import functools
import math

import jax
import jax.numpy as jnp
from jax import lax
from jax.experimental import pallas as pl
from jax.experimental.pallas import tpu as pltpu
from jax.sharding import PartitionSpec as P

CUBIC = 0.044715
ROOT = 0.7978845608028654
MESH = pl.DeviceIdType.MESH
F32 = jnp.float32
BF16 = jnp.bfloat16
LANES = 128
HALF_ROWS = 48


def dot_nn(a, b):
    return jnp.dot(a, b, preferred_element_type=F32)


def dot_nt(a, b):
    return lax.dot_general(a, b, (((1,), (1,)), ((), ())), preferred_element_type=F32)


def power(exponent):
    near = jnp.exp2(exponent)
    spread = near * float(2**16 + 1)
    return spread - (spread - near)


def kernel(
    members_n, spaces_n, chan,
    x_hbm, w_hbm, bias_hbm, wo_hbm, mem_hbm, tgt_hbm, area_hbm,
    ig, owned,
    x, bias_ref, area_ref, stage, wo_raw, wo_wide, wall, wt, bias_b, mem, flat, packed, got, values,
    tgt_raw, tgt, grads, back, og, act, slope, pg, acc_in, acc_out, acc_b, part, pair, total, shares,
    load_sem, w_recv, w_send, a2a_recv, a2a_send, a2a_own, back_recv, back_send, back_own,
    pair_sem, red_recv, red_send, fin_recv, fin_send,
):
    me = lax.axis_index("member")
    here = lax.axis_index("space")
    core = lax.rem(me, 2)
    own_m, hid, cells = ig.shape
    rows = w_hbm.shape[0]
    half_spaces = spaces_n // 2
    half_members = members_n // 2
    half_hid = hid // 2
    half_cells = cells // 2
    count = own_m * members_n
    wide = wt.shape[0]
    half_chan = (chan + 1) // 2
    words = own_m - 1
    my_half = lax.rem(here // half_spaces + core, 2)
    sibling = me + 1 - 2 * core

    def member_peer(k):
        return lax.rem(me + k, members_n)

    def space_peer(k):
        return my_half * half_spaces + lax.rem(here + k, half_spaces)

    far_first = sorted(range(1, members_n), key=lambda k: -min(k, members_n - k))
    barrier = pltpu.get_barrier_semaphore()

    def greet_space(k, _):
        pl.semaphore_signal(barrier, inc=1, device_id={"space": space_peer(k)}, device_id_type=MESH)
        return 0

    def greet_member(k, _):
        pl.semaphore_signal(barrier, inc=1, device_id={"member": member_peer(k)}, device_id_type=MESH)
        return 0

    first = 1 - core
    lax.fori_loop(first, half_spaces, greet_space, 0)
    lax.fori_loop(1, members_n, greet_member, 0)

    load_w = pltpu.make_async_copy(w_hbm, stage.at[:, 0:wide], load_sem.at[own_m])
    load_wo = pltpu.make_async_copy(wo_hbm, wo_raw, load_sem.at[own_m + 1])
    load_tgt = pltpu.make_async_copy(tgt_hbm, tgt_raw, load_sem.at[own_m + 2])
    load_bias = pltpu.make_async_copy(bias_hbm, bias_ref, load_sem.at[own_m + 3])
    load_area = pltpu.make_async_copy(area_hbm, area_ref, load_sem.at[own_m + 4])

    def columns(chunk, m, members=1):
        start = (chunk * own_m + m) * half_cells
        return slice(start, start + members * half_cells)

    loads = [
        pltpu.make_async_copy(
            x_hbm.at[m, :, chunk * half_cells : (chunk + 1) * half_cells],
            x.at[:, columns(chunk, m)],
            load_sem.at[m if chunk == 0 else own_m + 5 + members_n + m],
        )
        for chunk in range(2)
        for m in range(own_m)
    ]
    load_mem = [
        pltpu.make_async_copy(
            mem_hbm.at[:, :, t * LANES : (t + 1) * LANES], mem.at[t], load_sem.at[own_m + 5 + t]
        )
        for t in range(members_n)
    ]
    for load in load_mem:
        load.start()
    load_w.start()
    load_wo.start()
    load_tgt.start()
    load_bias.start()
    load_area.start()
    for load in loads:
        load.start()

    wo_wide[...] = jnp.zeros(wo_wide.shape, F32)
    load_wo.wait()
    wo_wide[:, 0:half_chan] = wo_raw[:, 0:half_chan].astype(F32)
    second = HALF_ROWS + 2 * half_chan - chan
    wo_wide[:, second : second + chan - half_chan] = wo_raw[:, half_chan:chan].astype(F32)
    stage[:, wide:] = wo_wide[...].astype(BF16)
    load_w.wait()

    def place(peer, chunk):
        channel_half = lax.rem(peer // half_members + chunk, 2)
        tile = lax.rem(peer, half_members) + chunk * half_members
        return channel_half, pl.ds(pl.multiple_of(tile * LANES, LANES), LANES)

    flat[half_chan * own_m :, :] = jnp.zeros((flat.shape[0] - half_chan * own_m, LANES), F32)

    def encode(chunk):
        def step(peer, _):
            channel_half, _ = place(peer, chunk)
            tile = lax.rem(peer, half_members) + chunk * half_members
            start = channel_half * (chan - half_chan)
            for c in range(half_chan):
                flat[c * own_m : (c + 1) * own_m, :] = mem[tile, start + c]
            for i in reversed(range(HALF_ROWS // 8)):
                whole = [
                    flat[pl.ds(i * 8 * own_m + m, 8, stride=own_m), :] * float(2**18) for m in range(own_m)
                ]
                code = whole[words] - float(2**21)
                size = jnp.abs(code)
                digit2 = jnp.floor(size * (1.0 / 2**14))
                size = size - digit2 * float(2**14)
                digit1 = jnp.floor(size * (1.0 / 2**7))
                digits = (size - digit1 * float(2**7), digit1, digit2)
                for j in range(words):
                    word = (whole[j] + float(2**23)) * power(digits[j] - 64.0)
                    if j == words - 1:
                        word = jnp.where(code < 0.0, -word, word)
                    packed[chunk, peer, j * half_chan + i * 8 : j * half_chan + (i + 1) * 8, :] = word
            return 0

        lax.fori_loop(0, members_n, step, 0)

    def decode(chunk):
        def step(source, _):
            for i in range(HALF_ROWS // 8):
                rank_rows = slice(i * 8, (i + 1) * 8)
                digits = [None] * words
                for j in range(words):
                    word = got[chunk, source, j * half_chan + i * 8 : j * half_chan + (i + 1) * 8, :]
                    size = jnp.abs(word) if j == words - 1 else word
                    digits[j] = jnp.floor(jnp.log2(size) + 0.2) + (64.0 - 23.0)
                    values[source * own_m + j, rank_rows, :] = size * power(64.0 - digits[j]) - float(2**23)
                code = (digits[2] * 128.0 + digits[1]) * 128.0 + digits[0]
                values[source * own_m + words, rank_rows, :] = jnp.where(word < 0.0, -code, code) + float(2**21)
            return 0

        lax.fori_loop(0, members_n, step, 0)

    def values_to(k, chunk):
        peer = member_peer(k)
        return pltpu.make_async_remote_copy(
            src_ref=packed.at[chunk, peer],
            dst_ref=got.at[chunk, me],
            send_sem=a2a_send.at[chunk],
            recv_sem=a2a_recv.at[chunk],
            device_id={"member": peer},
            device_id_type=MESH,
        )

    def own_values(chunk):
        return pltpu.make_async_copy(packed.at[chunk, me], got.at[chunk, me], a2a_own.at[chunk])

    def send_values(chunk):
        for k in far_first:
            values_to(k, chunk).start()
        own_values(chunk).start()

    def values_sent(chunk):
        rest = got.at[chunk, 0 : members_n - 1]
        pltpu.make_async_copy(rest, rest, a2a_send.at[chunk]).wait()

    def send_rows(k, _):
        pltpu.make_async_remote_copy(
            src_ref=stage, dst_ref=wall.at[here], send_sem=w_send.at[0], recv_sem=w_recv.at[0],
            device_id={"space": space_peer(k)}, device_id_type=MESH,
        ).start()
        return 0

    for load in load_mem:
        load.wait()
    encode(0)
    encode(1)
    pl.semaphore_wait(barrier, members_n - 1 + half_spaces - first)
    send_values(0)
    send_values(1)
    lax.fori_loop(first, half_spaces, send_rows, 0)

    @pl.when(core == 0)
    def _():
        pltpu.make_async_copy(stage, wall.at[here], w_recv.at[0]).start()


    load_bias.wait()
    load_area.wait()
    bias_b[...] = jnp.broadcast_to(bias_ref[...], (LANES, hid)).T
    og[:, 2 * HALF_ROWS :, :] = jnp.zeros((own_m, og.shape[1] - 2 * HALF_ROWS, cells), BF16)
    tgt[...] = jnp.zeros(tgt.shape, F32)
    acc_b[...] = jnp.zeros(acc_b.shape, F32)
    load_tgt.wait()
    tgt[0, 0:half_chan, :] = tgt_raw[0:half_chan, :] * float(2**18)
    tgt[1, 0:half_chan, :] = tgt_raw[chan - half_chan : chan, :] * float(2**18)

    mine_w = wall.at[pl.ds(my_half * half_spaces, half_spaces)]
    pltpu.make_async_copy(mine_w, mine_w, w_recv.at[0]).wait()
    pair_w = pltpu.make_async_remote_copy(
        src_ref=mine_w, dst_ref=mine_w, send_sem=w_send.at[1], recv_sem=w_recv.at[1],
        device_id={"member": sibling}, device_id_type=MESH,
    )
    pair_w.start()

    group = 8

    def rank(chunk):
        own_values(chunk).wait()
        rest = got.at[chunk, 0 : members_n - 1]
        pltpu.make_async_copy(rest, rest, a2a_recv.at[chunk]).wait()
        channel_half, at = place(me, chunk)
        area_row = area_ref[:, at] * (1.0 / count)

        decode(chunk)

        def rank_rows(tile, _):
            eight = pl.ds(pl.multiple_of(tile * 8, 8), 8)

            def value(k):
                return values[k, eight, :]

            for one in range(0, count, group):
                left = [value(one + i) for i in range(group)]
                for other in range(one, count, group):
                    right = left if other == one else [value(other + i) for i in range(group)]
                    up = [None] * group
                    down = [None] * group
                    for i in range(group):
                        for j in range(i + 1 if other == one else 0, group):
                            above = jnp.where(left[i] > right[j], 1.0, 0.0)
                            up[i] = above if up[i] is None else up[i] + above
                            down[j] = above if down[j] is None else down[j] + above
                    for i in range(group):
                        if other == one:
                            less = float(i)
                            if up[i] is not None:
                                less = less + up[i]
                            if down[i] is not None:
                                less = less - down[i]
                            grads[one + i, eight, :] = less if one == 0 else grads[one + i, eight, :] + less
                        else:
                            grads[one + i, eight, :] += up[i]
                            below = float(group) - down[i]
                            grads[other + i, eight, :] = below if one == 0 else grads[other + i, eight, :] + below
            target = tgt[channel_half, eight, at]
            for k in range(count):
                grad = jnp.where(value(k) > target, float(2 * (count - 1)), 0.0) - 2.0 * grads[k, eight, :]
                grads[k, eight, :] = grad * area_row
            return 0

        lax.fori_loop(0, HALF_ROWS // 8, rank_rows, 0)

        def pack(k, _):
            back[chunk, k] = grads[k].astype(BF16)
            return 0

        lax.fori_loop(0, count, pack, 0)

    def send_grads(chunk):
        for k in far_first:
            grads_to(k, chunk).start()
        own_grads(chunk).start()

    def grads_place(chunk):
        channel_half, at = place(me, chunk)
        return og.at[:, pl.ds(pl.multiple_of(channel_half * HALF_ROWS, HALF_ROWS), HALF_ROWS), at]

    def grads_to(k, chunk):
        peer = member_peer(k)
        return pltpu.make_async_remote_copy(
            src_ref=back.at[chunk, pl.ds(peer * own_m, own_m)],
            dst_ref=grads_place(chunk),
            send_sem=back_send.at[chunk],
            recv_sem=back_recv.at[chunk],
            device_id={"member": peer},
            device_id_type=MESH,
        )

    def own_grads(chunk):
        return pltpu.make_async_copy(
            back.at[chunk, pl.ds(me * own_m, own_m)], grads_place(chunk), back_own.at[chunk]
        )

    def wait_grads(chunk):
        own_grads(chunk).wait()
        rest = back.at[chunk, 0 : count - own_m]
        pltpu.make_async_copy(rest, rest, back_recv.at[chunk]).wait()

    rank(0)
    values_sent(1)
    send_grads(0)

    pair_w.wait_recv()

    def weights():
        return wall[...].reshape(hid, wide + LANES)

    wt[...] = weights()[:, 0:wide].T

    def cut(chunk):
        return slice(chunk * half_cells, (chunk + 1) * half_cells)


    def forward(chunk):
        at = cut(chunk)
        bias2 = jnp.concatenate([bias_b[...]] * (half_cells // LANES), axis=1)
        for m in range(own_m):
            v = dot_nn(wt[...], x[:, columns(chunk, m)]) + bias2
            sq = v * v
            u = 0.5 + 0.5 * jnp.tanh(v * (ROOT + (ROOT * CUBIC) * sq))
            a = v * u
            act[m, :, at] = a.astype(BF16)
            slope[m, :, at] = (u + a * (1.0 - u) * (2.0 * ROOT + (6.0 * ROOT * CUBIC) * sq)).astype(BF16)

    for load in loads:
        load.wait()
    forward(0)
    rank(1)
    send_grads(1)
    forward(1)

    def pre_grads(chunk):
        at = cut(chunk)
        wop = weights()[:, wide:]
        for m in range(own_m):
            p = dot_nn(wop, og[m, :, at]) * slope[m, :, at].astype(F32)
            pg[:, columns(chunk, m)] = p.astype(BF16)
            folded = p[:, 0:LANES]
            for c in range(1, half_cells // LANES):
                folded = folded + p[:, c * LANES : (c + 1) * LANES]
            acc_b[...] += folded

    def terms_in(chunk, of):
        every = columns(chunk, 0, own_m)
        return dot_nt(x[of, every], pg[:, every])

    def terms_out(chunk, of):
        at = cut(chunk)
        return functools.reduce(jnp.add, [dot_nt(act[m, of, at], og[m, :, at]) for m in range(own_m)])

    def input_grads(chunk):
        at = cut(chunk)

        def step(m, _):
            start = pl.multiple_of((chunk * own_m + m) * half_cells, half_cells)
            ig[m, :, at] = dot_nn(weights()[:, 0:wide], pg[:, pl.ds(start, half_cells)]).astype(BF16)
            return 0

        lax.fori_loop(0, own_m, step, 0)

    mine = pl.ds(pl.multiple_of(my_half * half_hid, half_hid), half_hid)
    theirs = pl.ds(pl.multiple_of((1 - my_half) * half_hid, half_hid), half_hid)

    wait_grads(0)
    pre_grads(0)
    for of in (slice(0, half_hid), slice(half_hid, hid)):
        acc_in[of, :] = terms_in(0, of)
        acc_out[of, :] = terms_out(0, of)
    wait_grads(1)
    pre_grads(1)

    last_lane = lax.broadcasted_iota(jnp.int32, (half_hid, LANES), 1) == LANES - 1

    def with_bias(of, terms):
        return jnp.where(last_lane, jnp.sum(acc_b[of, :], axis=1, keepdims=True), terms)

    part[:, 0:wide] = (acc_in[theirs, :] + terms_in(1, theirs)).astype(BF16)
    part[:, wide:] = with_bias(theirs, acc_out[theirs, :] + terms_out(1, theirs)).astype(BF16)
    to_sibling = pltpu.make_async_remote_copy(
        src_ref=part, dst_ref=pair, send_sem=pair_sem.at[0], recv_sem=pair_sem.at[1],
        device_id={"member": sibling}, device_id_type=MESH,
    )
    to_sibling.start()
    acc_in[mine, :] += terms_in(1, mine)
    acc_out[mine, :] = with_bias(mine, acc_out[mine, :] + terms_out(1, mine))
    to_sibling.wait_recv()
    total[:, 0:wide] = (acc_in[mine, :] + pair[:, 0:wide].astype(F32)).astype(BF16)
    total[:, wide:] = (acc_out[mine, :] + pair[:, wide:].astype(F32)).astype(BF16)

    slot = lax.rem(here, half_spaces)

    def send_block(k, _):
        block = lax.rem(here + k, half_spaces)
        pltpu.make_async_remote_copy(
            src_ref=total.at[pl.ds(pl.multiple_of(block * rows, rows), rows), :],
            dst_ref=shares.at[slot],
            send_sem=red_send, recv_sem=red_recv,
            device_id={"space": space_peer(k)}, device_id_type=MESH,
        ).start()
        return 0

    lax.fori_loop(first, half_spaces, send_block, 0)

    @pl.when(core == 0)
    def _():
        pltpu.make_async_copy(
            total.at[pl.ds(pl.multiple_of(slot * rows, rows), rows), :], shares.at[slot], red_recv
        ).start()

    input_grads(0)
    input_grads(1)

    pltpu.make_async_copy(shares, shares, red_recv).wait()
    value = shares[0].astype(F32)
    for k in range(1, half_spaces):
        value = value + shares[k].astype(F32)
    owned[me] = value.astype(BF16)

    for k in far_first:
        pltpu.make_async_remote_copy(
            src_ref=owned.at[me], dst_ref=owned.at[me], send_sem=fin_send, recv_sem=fin_recv,
            device_id={"member": member_peer(k)}, device_id_type=MESH,
        ).start()
    rest = owned.at[0 : members_n - 1]
    pltpu.make_async_copy(rest, rest, fin_recv).wait()
    values_sent(0)
    for chunk in range(2):
        rest = back.at[chunk, 0 : count - own_m]
        pltpu.make_async_copy(rest, rest, back_send.at[chunk]).wait()
    pair_w.wait_send()
    to_sibling.wait_send()
    rest = owned.at[0 : members_n - 1]
    pltpu.make_async_copy(rest, rest, fin_send).wait()

    def wait_sent(peers):
        rest = wall.at[0:peers]
        pltpu.make_async_copy(rest, rest, w_send.at[0]).wait()
        rest = shares.at[0:peers]
        pltpu.make_async_copy(rest, rest, red_send).wait()

    @pl.when(core == 0)
    def _():
        wait_sent(half_spaces - 1)

    @pl.when(core == 1)
    def _():
        wait_sent(half_spaces)


def finish(
    chan, scale, ig_ref, owned_ref, ig_out, win_out, wout_out, bias_out, win, wout, bias, sem
):
    copies = [pltpu.make_async_copy(ig_ref.at[m], ig_out.at[m], sem.at[m]) for m in range(ig_ref.shape[0])]
    for copy in copies:
        copy.start()
    members_n, rows, full = owned_ref.shape
    wide = full - LANES
    half_chan = (chan + 1) // 2
    result = owned_ref[0].astype(F32)
    for k in range(1, members_n):
        result = result + owned_ref[k].astype(F32)
    result = result * scale
    win[...] = result[:, 0:wide]
    wout[:, 0:half_chan] = result[:, wide : wide + half_chan]
    second = wide + HALF_ROWS + 2 * half_chan - chan
    wout[:, half_chan:chan] = result[:, second : second + chan - half_chan]
    diagonal = lax.broadcasted_iota(jnp.int32, (rows, rows), 0) == lax.broadcasted_iota(
        jnp.int32, (rows, rows), 1
    )
    bias[...] = jnp.sum(jnp.where(diagonal, result[:, full - 1 : full], 0.0), axis=0, keepdims=True)
    first = len(copies)
    for k, (source, out) in enumerate(((win, win_out), (wout, wout_out), (bias, bias_out))):
        copies.append(pltpu.make_async_copy(source, out, sem.at[first + k]))
        copies[-1].start()
    for copy in copies:
        copy.wait()


def body(members_n, spaces_n, inputs, w_in, bias_in, w_out, members_out, target, cell_area):
    own_m, hid, cells = inputs.shape
    rows, chan = w_out.shape
    wide = w_in.shape[1]
    count = own_m * members_n
    scale = 1.0 / math.sqrt(count * cells * spaces_n)
    half_chan = (chan + 1) // 2
    packed_rows = (own_m - 2) * half_chan + HALF_ROWS
    half_spaces = spaces_n // 2
    hbm_spec = pl.BlockSpec(memory_space=pltpu.HBM)
    vmem_spec = pl.BlockSpec(memory_space=pltpu.VMEM)
    dma = pltpu.SemaphoreType.DMA
    hidden = (own_m, hid, cells)
    full = wide + LANES
    operands = (
        inputs, w_in, bias_in.reshape(1, -1), w_out, members_out.transpose(1, 0, 2), target,
        cell_area.reshape(1, -1),
    )
    partial = pl.pallas_call(
        functools.partial(kernel, members_n, spaces_n, chan),
        out_shape=(pltpu.VMEM(hidden, BF16), pltpu.VMEM((members_n, rows, full), BF16)),
        in_specs=[hbm_spec] * 7,
        out_specs=(vmem_spec, vmem_spec),
        scratch_shapes=[
            pltpu.VMEM((hid, own_m * cells), BF16),
            pltpu.VMEM((1, hid), F32),
            pltpu.VMEM((1, cells), F32),
            pltpu.VMEM((rows, full), BF16),
            pltpu.VMEM((rows, chan), BF16),
            pltpu.VMEM((rows, LANES), F32),
            pltpu.VMEM((spaces_n, rows, full), BF16),
            pltpu.VMEM((wide, hid), BF16),
            pltpu.VMEM((hid, LANES), F32),
            pltpu.VMEM((members_n, chan, own_m, LANES), F32),
            pltpu.VMEM((HALF_ROWS * own_m, LANES), F32),
            pltpu.VMEM((2, members_n, packed_rows, LANES), F32),
            pltpu.VMEM((2, members_n, packed_rows, LANES), F32),
            pltpu.VMEM((count, HALF_ROWS, LANES), F32),
            pltpu.VMEM((chan, cells), F32),
            pltpu.VMEM((2, HALF_ROWS, cells), F32),
            pltpu.VMEM((count, HALF_ROWS, LANES), F32),
            pltpu.VMEM((2, count, HALF_ROWS, LANES), BF16),
            pltpu.VMEM((own_m, LANES, cells), BF16),
            pltpu.VMEM(hidden, BF16),
            pltpu.VMEM(hidden, BF16),
            pltpu.VMEM((hid, own_m * cells), BF16),
            pltpu.VMEM((hid, wide), F32),
            pltpu.VMEM((hid, LANES), F32),
            pltpu.VMEM((hid, LANES), F32),
            pltpu.VMEM((hid // 2, full), BF16),
            pltpu.VMEM((hid // 2, full), BF16),
            pltpu.VMEM((hid // 2, full), BF16),
            pltpu.VMEM((half_spaces, rows, full), BF16),
            dma((2 * own_m + 5 + members_n,)),
            dma((2,)),
            dma((2,)),
            dma((2,)),
            dma((2,)),
            dma((2,)),
            dma((2,)),
            dma((2,)),
            dma((2,)),
            dma((2,)),
            dma,
            dma,
            dma,
            dma,
        ],
        compiler_params=pltpu.CompilerParams(
            collective_id=0, has_side_effects=True, vmem_limit_bytes=48 * 1024 * 1024
        ),
        name="crps_backward",
    )(*(pltpu.with_memory_space_constraint(operand, pltpu.HBM) for operand in operands))
    input_grad, w_in_grad, w_out_grad, bias_grad = pl.pallas_call(
        functools.partial(finish, chan, scale),
        out_shape=(
            jax.ShapeDtypeStruct(hidden, BF16),
            jax.ShapeDtypeStruct((rows, wide), F32),
            jax.ShapeDtypeStruct((rows, chan), F32),
            jax.ShapeDtypeStruct((1, rows), F32),
        ),
        in_specs=[vmem_spec, vmem_spec],
        out_specs=(hbm_spec,) * 4,
        scratch_shapes=[
            pltpu.VMEM((rows, wide), F32),
            pltpu.VMEM((rows, chan), F32),
            pltpu.VMEM((1, rows), F32),
            dma((own_m + 3,)),
        ],
        compiler_params=pltpu.CompilerParams(vmem_limit_bytes=16 * 1024 * 1024),
        name="finish",
    )(*(pltpu.with_memory_space_constraint(array, pltpu.VMEM) for array in partial))
    return input_grad, w_in_grad, w_out_grad, bias_grad.reshape(rows)


def solution(mesh):
    members_n, spaces_n = mesh.shape["member"], mesh.shape["space"]
    return jax.shard_map(
        functools.partial(body, members_n, spaces_n),
        mesh=mesh,
        in_specs=(
            P("member", None, "space"),
            P("space", None),
            P(),
            P("space", None),
            P("member", None, "space"),
            P(None, "space"),
            P("space"),
        ),
        out_specs=(P("member", None, "space"), P("space", None), P("space", None), P("space")),
        check_vma=False,
    )
```
